32 devices in a mesh: space: 8 (over z, x), sub: 4 (over y, core).
Axes of the slice: x: 2, y: 2, z: 4, core: 2. Of those that a mesh axis runs over, the one named last changes fastest.
Arguments:
- offsets: float32 [8, 4, 8, 4, 4, 3, 128], P('space', 'sub'), may hold values from 0.5 to 7.5
- normals: float32 [8, 4, 8, 4, 4, 3, 128], P('space', 'sub'), may hold values from -6 to 6
- density: float32 [8, 4, 8, 4, 4, 128], P('space', 'sub'), may hold values from 0.3 to 3
- tile_brick: int32 [8, 4, 8, 4, 4], P('space', 'sub'), may hold values from 0 to 63
- tile_count: int32 [8, 4, 8, 4, 4], P('space', 'sub'), may hold values from 32 to 128, as said below
Outputs:
- indicator: float32 [128, 64, 128], P('space', 'sub')
- density_field: float32 [128, 64, 128], P('space', 'sub')
The draws below stay inside these ranges and needn't reach their ends.
Inputs may be any that keep to these rules, and one draw needn't show every extreme that they name: `tile_count`: slots at and beyond a tile's count are padding; some tile holds 128 live points.
All inputs are finite; a program needn't handle non-finite values.
Results may differ from the reference program's by a relative error of at most 0.0003.
Values sent between devices are 32-bit elements; how exact they have to be, the bound alone decides.
A program may use at most 192 MiB of HBM per device.

```python
import math
import jax
import jax.numpy as jnp
from jax import lax

BRICK = 8
SLOTS = 128
TPD = 4
CX = 16
CY = 16
CZ = 128
LEVELS = 4
SWEEPS = 2
COARSE = 8
NX = 128
NY = 64
NZ = 128
BR_DEV = 64
N_SPACE = 8
N_SUB = 4


def draw_tile_count(key, part):
    counts = jax.random.randint(key, (N_SPACE, N_SUB, N_SPACE, N_SUB, TPD), SLOTS // 4, SLOTS + 1)
    return counts.astype(jnp.int32).at[0, 0, 0, 0, 0].set(SLOTS)


def with_ends(values, rng, smallest, largest):
    place = [jax.random.randint(jax.random.fold_in(rng, axis), (), 0, length) for axis, length in enumerate(values.shape)]
    widest = values.shape.index(max(values.shape))
    next_to = place[:widest] + [(place[widest] + 1) % values.shape[widest]] + place[widest + 1:]
    return values.at[tuple(place)].set(smallest).at[tuple(next_to)].set(largest)


def steps_of(rng, dims, shards, smallest, high):
    factor_of, own = 1.0, jax.random.fold_in(rng, 6)
    for axis_at, shards_of in shards:
        heights = jnp.exp(jax.random.uniform(jax.random.fold_in(own, axis_at), (shards_of,), jnp.float32, smallest / len(shards), high / len(shards)))
        factor_of = factor_of * jnp.repeat(heights, dims[axis_at] // shards_of).reshape([-1 if axis == axis_at else 1 for axis in range(len(dims))])
    return factor_of


def centred(own_key, extent, width, most, pieces=(), held_as=jnp.bfloat16):
    gain = steps_of(own_key, extent, pieces, -0.22, 0.18) if pieces else 1.0
    values = jax.random.normal(own_key, extent, jnp.float32) * width * gain
    return jnp.minimum(jnp.maximum(values, -most), most).astype(held_as)


def setup_inputs(seed: int = 0) -> dict:
    keys = jax.random.split(jax.random.key(seed), 6)
    offsets = jnp.clip(0.5 + 7.0 * jax.random.uniform(keys[0], (N_SPACE, N_SUB, N_SPACE, N_SUB, TPD, 3, SLOTS), jnp.float32) ** steps_of(keys[0], (N_SPACE, N_SUB, N_SPACE, N_SUB, TPD, 3, SLOTS), ((0, 8), (1, 4)), -0.2, 0.2), 0.5, 7.5)
    normals = centred(keys[1], (N_SPACE, N_SUB, N_SPACE, N_SUB, TPD, 3, SLOTS), 1.0, 6.0, ((0, 8), (1, 4)), jnp.float32)
    density = jnp.clip(jnp.exp(math.log(3.0) - 2.3025851 * jax.random.uniform(keys[2], (N_SPACE, N_SUB, N_SPACE, N_SUB, TPD, SLOTS), jnp.float32) ** steps_of(keys[2], (N_SPACE, N_SUB, N_SPACE, N_SUB, TPD, SLOTS), ((0, 8), (1, 4)), -0.2, 0.2)), 0.3, 3.0)
    tile_brick = with_ends(jax.random.randint(keys[3], (N_SPACE, N_SUB, N_SPACE, N_SUB, TPD), 0, BR_DEV), jax.random.fold_in(keys[3], 1), 0, BR_DEV - 1).astype(jnp.int32)
    tile_count = draw_tile_count(jax.random.fold_in(keys[5], 71), 0)
    return {"offsets": offsets, "normals": normals, "density": density, "tile_brick": tile_brick, "tile_count": tile_count}


screen_weight = 0.05
relax_weight = 0.8


def splat_tiles(offsets_tile, samples_tile):
    tile_total = offsets_tile.shape[0]
    slot_total = offsets_tile.shape[2]
    centers = jnp.arange(BRICK, dtype=jnp.float32) + 0.5
    weights = jnp.maximum(0.0, 1.0 - jnp.abs(offsets_tile[:, :, None, :] - centers[None, None, :, None]))
    planar = (weights[:, 0, :, None, :] * weights[:, 1, None, :, :]).reshape(tile_total, BRICK * BRICK, slot_total)
    loaded = (samples_tile[:, :, None, :] * weights[:, 2][:, None, :, :]).reshape(tile_total, 4 * BRICK, slot_total)
    result = jnp.einsum("tas,tbs->tab", planar, loaded, precision=lax.Precision.HIGHEST)
    return result.reshape(tile_total, -1)


def to_grid(sums):
    shaped = sums.reshape(CX // BRICK, CY // BRICK, CZ // BRICK, BRICK, BRICK, 4, BRICK)
    return shaped.transpose(5, 0, 3, 1, 4, 2, 6).reshape(4, CX, CY, CZ)


def neighbours(padded):
    total = padded[2:, 1:-1, 1:-1] + padded[:-2, 1:-1, 1:-1]
    total = total + padded[1:-1, 2:, 1:-1] + padded[1:-1, :-2, 1:-1]
    return total + padded[1:-1, 1:-1, 2:] + padded[1:-1, 1:-1, :-2]


def operate(field, screen, level_index):
    return (6.0 * field - neighbours(jnp.pad(field, 1))) * (0.25 ** level_index) + screen * field


def sweep(field, forcing, screen, diagonal, level_index):
    return field + relax_weight * (forcing - operate(field, screen, level_index)) / diagonal


def restrict(field):
    sx, sy, sz = field.shape
    return field.reshape(sx // 2, 2, sy // 2, 2, sz // 2, 2).mean(axis=(1, 3, 5))


def prolong(field):
    return jnp.repeat(jnp.repeat(jnp.repeat(field, 2, axis=0), 2, axis=1), 2, axis=2)


def vcycle(forcing, level_index, screens):
    screen = screens[level_index]
    diagonal = 6.0 * (0.25 ** level_index) + screen
    field = relax_weight * forcing / diagonal
    if level_index == LEVELS - 1:
        for sweep_index in range(COARSE - 1):
            field = sweep(field, forcing, screen, diagonal, level_index)
        return field
    for sweep_index in range(SWEEPS - 1):
        field = sweep(field, forcing, screen, diagonal, level_index)
    residual = forcing - operate(field, screen, level_index)
    correction = vcycle(restrict(residual), level_index + 1, screens)
    field = field + prolong(correction)
    for sweep_index in range(SWEEPS):
        field = sweep(field, forcing, screen, diagonal, level_index)
    return field


def reference(offsets, normals, density, tile_brick, tile_count):
    brick_total = (CX // BRICK) * (CY // BRICK) * (CZ // BRICK)

    def pick(array, target_space, target_sub):
        first = lax.dynamic_index_in_dim(array, target_space, 2, keepdims=False)
        return lax.dynamic_index_in_dim(first, target_sub, 2, keepdims=False)

    def one_target(target):
        target_space = target // N_SUB
        target_sub = target % N_SUB
        offsets_here = pick(offsets, target_space, target_sub).reshape(-1, 3, SLOTS)
        normals_here = pick(normals, target_space, target_sub).reshape(-1, 3, SLOTS)
        density_here = pick(density, target_space, target_sub).reshape(-1, 1, SLOTS)
        counts_here = pick(tile_count, target_space, target_sub).reshape(-1)
        bricks_here = pick(tile_brick, target_space, target_sub).reshape(-1)
        live_slots = (jnp.arange(SLOTS, dtype=jnp.int32)[None, :] < counts_here[:, None]).astype(jnp.float32)
        samples = jnp.concatenate([normals_here, density_here], axis=1) * live_slots[:, None, :]
        partials = splat_tiles(offsets_here, samples)
        onehot = (bricks_here[None, :] == jnp.arange(brick_total, dtype=jnp.int32)[:, None]).astype(jnp.float32)
        sums = jnp.dot(onehot, partials, precision=lax.Precision.HIGHEST, preferred_element_type=jnp.float32)
        return to_grid(sums)

    blocks = lax.map(one_target, jnp.arange(N_SPACE * N_SUB, dtype=jnp.int32))
    grid = blocks.reshape(N_SPACE, N_SUB, 4, CX, CY, CZ).transpose(2, 0, 3, 1, 4, 5).reshape(4, NX, NY, NZ)
    density_field = grid[3]
    padded_x = jnp.pad(grid[0], ((1, 1), (0, 0), (0, 0)))
    padded_y = jnp.pad(grid[1], ((0, 0), (1, 1), (0, 0)))
    padded_z = jnp.pad(grid[2], ((0, 0), (0, 0), (1, 1)))
    change = (padded_x[2:] - padded_x[:-2]) + (padded_y[:, 2:] - padded_y[:, :-2])
    change = change + (padded_z[:, :, 2:] - padded_z[:, :, :-2])
    forcing = -0.5 * change
    screens = []
    rho_level = density_field
    for level_index in range(LEVELS):
        screens.append(screen_weight * rho_level)
        rho_level = restrict(rho_level) if level_index < LEVELS - 1 else rho_level
    indicator = vcycle(forcing, 0, screens)
    return indicator, density_field
```

```python
import functools
import math

import jax
import jax.numpy as jnp
from jax import lax
from jax.experimental import pallas as pl
from jax.experimental.pallas import tpu as pltpu
from jax.sharding import PartitionSpec as P

BRICK = 8
CX = 16
CY = 16
CZ = 128
LEVELS = 4
SWEEPS = 2
COARSE = 8


screen_weight = 0.05
relax_weight = 0.8


def splat_tiles(offsets_tile, samples_tile):
    tile_total = offsets_tile.shape[0]
    slot_total = offsets_tile.shape[2]
    centers = jnp.arange(BRICK, dtype=jnp.float32) + 0.5
    weights = jnp.maximum(
        0.0, 1.0 - jnp.abs(offsets_tile[:, :, None, :] - centers[None, None, :, None])
    )
    planar = (weights[:, 0, :, None, :] * weights[:, 1, None, :, :]).reshape(
        tile_total, BRICK * BRICK, slot_total
    )
    loaded = (samples_tile[:, :, None, :] * weights[:, 2][:, None, :, :]).reshape(
        tile_total, 4 * BRICK, slot_total
    )
    result = jnp.einsum("tas,tbs->tab", planar, loaded, precision=lax.Precision.HIGHEST)
    return result.reshape(tile_total, -1)


def splat_blocks(offsets_flat, samples_flat):
    tile_total = offsets_flat.shape[0]
    block_size = math.gcd(tile_total, 64)
    slot_total = offsets_flat.shape[2]

    def one_block(inputs):
        return splat_tiles(inputs[0], inputs[1])

    result = lax.map(
        one_block,
        (
            offsets_flat.reshape(tile_total // block_size, block_size, 3, slot_total),
            samples_flat.reshape(tile_total // block_size, block_size, 4, slot_total),
        ),
    )
    return result.reshape(tile_total, -1)


def to_grid(sums):
    shaped = sums.reshape(CX // BRICK, CY // BRICK, CZ // BRICK, BRICK, BRICK, 4, BRICK)
    return shaped.transpose(5, 0, 3, 1, 4, 2, 6).reshape(4, CX, CY, CZ)


HX = 4
HY = 8
MESH = pl.DeviceIdType.MESH
HIGHEST = lax.Precision.HIGHEST


def dot(a, b):
    return jnp.dot(a, b, precision=HIGHEST, preferred_element_type=jnp.float32)


def grid_iota(shape):
    return lax.broadcasted_iota(jnp.int32, shape, 0), lax.broadcasted_iota(jnp.int32, shape, 1)


def one_where(mask, value=1.0):
    return jnp.where(mask, jnp.float32(value), jnp.float32(0.0))


def shifted_z(c, zero_ends):
    zp = pltpu.roll(c, 127, c.ndim - 1)
    zm = pltpu.roll(c, 1, c.ndim - 1)
    if zero_ends:
        lane = lax.broadcasted_iota(jnp.int32, c.shape, c.ndim - 1)
        zp = jnp.where(lane < 127, zp, 0.0)
        zm = jnp.where(lane > 0, zm, 0.0)
    return zp + zm


def plane_neighbours(ref, x, zero_ends):
    c = ref[x]
    rows = c.shape[0]
    total = ref[x - 1] + ref[x + 1]
    total = total + pltpu.roll(c, 1, 0) + pltpu.roll(c, rows - 1, 0)
    return c, total + shifted_z(c, zero_ends)


def flat_neighbours(u, xs, zl, yl):
    row, lane = grid_iota(u.shape)
    rows = u.shape[0]
    xi, zi, yi = row % xs, lane % zl, lane // zl
    total = jnp.where(zi < zl - 1, pltpu.roll(u, 127, 1), 0.0)
    total = total + jnp.where(zi > 0, pltpu.roll(u, 1, 1), 0.0)
    total = total + jnp.where(xi < xs - 1, pltpu.roll(u, rows - 1, 0), 0.0)
    total = total + jnp.where(xi > 0, pltpu.roll(u, 1, 0), 0.0)
    far_up = pltpu.roll(pltpu.roll(u, zl * (yl - 1), 1), rows - xs, 0)
    far_up = jnp.where(row < rows - xs, far_up, 0.0)
    total = total + jnp.where(yi < yl - 1, pltpu.roll(u, 128 - zl, 1), far_up)
    far_down = pltpu.roll(pltpu.roll(u, 128 - zl * (yl - 1), 1), xs, 0)
    far_down = jnp.where(row >= xs, far_down, 0.0)
    return total + jnp.where(yi > 0, pltpu.roll(u, zl, 1), far_down)


class Halo:
    def __init__(self, ref, nx, ny, send, recv, base, has, place):
        self.ref, self.nx, self.ny = ref, nx, ny
        self.has = has
        self.items = []
        k = base
        for dx in (-1, 0, 1):
            for dy in (-1, 0, 1):
                if dx == 0 and dy == 0:
                    continue
                sx = {1: (nx, HX), -1: (HX, HX), 0: (HX, nx)}[dx]
                tx = {1: (0, HX), -1: (HX + nx, HX), 0: (HX, nx)}[dx]
                sy = {1: (ny, HY), -1: (HY, HY), 0: (HY, ny)}[dy]
                ty = {1: (0, HY), -1: (HY + ny, HY), 0: (HY, ny)}[dy]
                copy = pltpu.make_async_remote_copy(
                    src_ref=ref.at[pl.ds(*sx), pl.ds(*sy)],
                    dst_ref=ref.at[pl.ds(*tx), pl.ds(*ty)],
                    send_sem=send.at[k],
                    recv_sem=recv.at[k],
                    device_id=place(dx, dy),
                    device_id_type=MESH,
                )
                self.items.append((dx, dy, copy))
                k += 1

    def clear_rim(self):
        ref, nx, ny = self.ref, self.nx, self.ny

        @pl.when(jnp.logical_not(self.has(-1, 0)))
        def _():
            ref[0:HX] = jnp.zeros((HX,) + ref.shape[1:], jnp.float32)

        @pl.when(jnp.logical_not(self.has(1, 0)))
        def _():
            ref[HX + nx :] = jnp.zeros((HX,) + ref.shape[1:], jnp.float32)

        @pl.when(jnp.logical_not(self.has(0, -1)))
        def _():
            ref[:, 0:HY] = jnp.zeros((ref.shape[0], HY, 128), jnp.float32)

        @pl.when(jnp.logical_not(self.has(0, 1)))
        def _():
            ref[:, HY + ny :] = jnp.zeros((ref.shape[0], HY, 128), jnp.float32)

    def start(self):
        for dx, dy, copy in self.items:
            pl.when(self.has(dx, dy))(copy.start)

    def wait_recv(self):
        for dx, dy, copy in self.items:
            pl.when(self.has(-dx, -dy))(copy.wait_recv)

    def wait_send(self):
        for dx, dy, copy in self.items:
            pl.when(self.has(dx, dy))(copy.wait_send)


def planes(start, stop, unroll=2):
    def wrap(body):
        def step(x, carry):
            body(x)
            return carry

        lax.fori_loop(start, stop, step, 0, unroll=unroll)

    return wrap


def cycle_kernel(
    ns, nb, g, out,
    vxp, vyp, rhop, fp, ua, ub, wf, ws, rt,
    rho1p, f1p, u1a, u1b, wf1, ws1, rt1, pr,
    gsend, gath, f2g, rho2g, u2p, c2,
    send, recv, gsend_sem, grecv_sem,
):
    n = ns * nb
    sp, sb = lax.axis_index("space"), lax.axis_index("sub")
    me = sp * nb + sb

    def place(dx, dy):
        return (lax.rem(sp + dx + ns, ns), lax.rem(sb + dy + nb, nb))

    def has(dx, dy):
        ok = jnp.bool_(True)
        if dx:
            ok = sp + dx >= 0 if dx < 0 else sp + dx < ns
        if dy:
            oky = sb + dy >= 0 if dy < 0 else sb + dy < nb
            ok = jnp.logical_and(ok, oky) if dx else oky
        return ok

    barrier = pltpu.get_barrier_semaphore()

    def greet(k, carry):
        peer = lax.rem(me + k, n)
        pl.semaphore_signal(
            barrier, inc=1, device_id=(peer // nb, lax.rem(peer, nb)), device_id_type=MESH
        )
        return carry

    lax.fori_loop(1, n, greet, 0)

    rho_halo = Halo(rhop, 16, 16, send, recv, 0, has, place)
    f_halo = Halo(fp, 16, 16, send, recv, 8, has, place)
    rho1_halo = Halo(rho1p, 8, 8, send, recv, 16, has, place)
    f1_halo = Halo(f1p, 8, 8, send, recv, 24, has, place)

    def face(src, dst, k, dx, dy):
        return (
            dx,
            dy,
            pltpu.make_async_remote_copy(
                src_ref=src,
                dst_ref=dst,
                send_sem=send.at[k],
                recv_sem=recv.at[k],
                device_id=place(dx, dy),
                device_id_type=MESH,
            ),
        )

    faces = [
        face(vxp.at[16], vxp.at[0], 32, 1, 0),
        face(vxp.at[1], vxp.at[17], 33, -1, 0),
        face(vyp.at[:, pl.ds(16, 8)], vyp.at[:, pl.ds(0, 8)], 34, 0, 1),
        face(vyp.at[:, pl.ds(8, 8)], vyp.at[:, pl.ds(24, 8)], 35, 0, -1),
    ]
    vxp[1:17] = g[0]
    vyp[:, 8:24] = g[1]
    rhop[4:20, 8:24] = g[3]
    for halo in (rho_halo, f_halo, rho1_halo, f1_halo):
        halo.clear_rim()

    @pl.when(jnp.logical_not(has(-1, 0)))
    def _():
        vxp[0] = jnp.zeros((16, 128), jnp.float32)

    @pl.when(jnp.logical_not(has(1, 0)))
    def _():
        vxp[17] = jnp.zeros((16, 128), jnp.float32)

    @pl.when(jnp.logical_not(has(0, -1)))
    def _():
        vyp[:, 0:8] = jnp.zeros((16, 8, 128), jnp.float32)

    @pl.when(jnp.logical_not(has(0, 1)))
    def _():
        vyp[:, 24:32] = jnp.zeros((16, 8, 128), jnp.float32)

    zr, zc = grid_iota((128, 128))
    pool_z = one_where(zr // 2 == zc, 0.125)

    def pool_to_1(dst):
        pooled = rt[:, pl.ds(8, 8, stride=2), :] + rt[:, pl.ds(9, 8, stride=2), :]
        dst[4:12, 8:16] = dot(pooled.reshape(64, 128), pool_z).reshape(8, 8, 128)

    pool_lanes = one_where(zr // 2 == zc % 32, 0.125)
    prow = lax.broadcasted_iota(jnp.int32, (4, 8, 128), 1)
    plane_lane = lax.broadcasted_iota(jnp.int32, (4, 8, 128), 2)
    pick_rows = plane_lane // 32 == prow // 2

    def pool_to_2(value):
        spread = dot(value.reshape(32, 128), pool_lanes).reshape(4, 8, 128)
        return jnp.sum(jnp.where(pick_rows, spread, 0.0), axis=1)

    pl.semaphore_wait(barrier, n - 1)
    for dx, dy, copy in faces:
        pl.when(has(dx, dy))(copy.start)
    rho_halo.start()

    @planes(0, 8)
    def _(x):
        rt[x, 8:24] = g[3, 2 * x] + g[3, 2 * x + 1]

    pool_to_1(rho1p)
    rho1_halo.start()
    for i in range(4):
        rt1[i, 8:16] = rho1p[4 + 2 * i, 8:16] + rho1p[5 + 2 * i, 8:16]
    gsend[4:8] = pool_to_2(rt1[:, 8:16])

    for dx, dy, copy in faces:
        pl.when(has(-dx, -dy))(copy.wait_recv)

    lane16 = lax.broadcasted_iota(jnp.int32, (16, 128), 1)

    @planes(0, 16)
    def _(x):
        change = vxp[x + 2] - vxp[x]
        change = change + (vyp[x, 9:25] - vyp[x, 7:23])
        vz = g[2, x]
        zp = jnp.where(lane16 < 127, pltpu.roll(vz, 127, 1), 0.0)
        zm = jnp.where(lane16 > 0, pltpu.roll(vz, 1, 1), 0.0)
        fp[x + 4, 8:24] = -0.5 * (change + (zp - zm))

    f_halo.start()
    rho_halo.wait_recv()

    def inside(x, rows, lanes, step):
        r, l = grid_iota((rows, 128))
        gx = sp * step + x - HX
        gy = sb * step + r - HY
        ok = jnp.logical_and(gy >= 0, gy < nb * step)
        ok = jnp.logical_and(ok, jnp.logical_and(gx >= 0, gx < ns * step))
        return jnp.logical_and(ok, l < lanes) if lanes < 128 else ok

    @planes(0, 24)
    def _(x):
        ws[x] = jnp.where(inside(x, 32, 128, 16), relax_weight / (6.0 + screen_weight * rhop[x]), 0.0)

    rho1_halo.wait_recv()

    @planes(0, 16)
    def _(x):
        ws1[x] = jnp.where(
            inside(x, 24, 64, 8), relax_weight / (1.5 + screen_weight * rho1p[x]), 0.0
        )

    f_halo.wait_recv()

    @planes(1, 23)
    def _(x):
        value = ws[x] * fp[x]
        wf[x] = value
        ua[x] = value

    def sweeps(src, dst, wf_ref, ws_ref, scale, start, stop, zero_ends):
        @planes(start, stop)
        def _(x):
            c, total = plane_neighbours(src, x, zero_ends)
            if scale != 1.0:
                total = scale * total
            dst[x] = (1.0 - relax_weight) * c + (wf_ref[x] + ws_ref[x] * total)

    sweeps(ua, ub, wf, ws, 1.0, 2, 22, True)

    @planes(0, 8, 1)
    def _(x):
        parts = []
        for k in range(2):
            at = 4 + 2 * x + k
            c, total = plane_neighbours(ub, at, True)
            parts.append(fp[at] - (6.0 + screen_weight * rhop[at]) * c + total)
        rt[x] = parts[0] + parts[1]

    pool_to_1(f1p)
    f1_halo.start()
    f1_halo.wait_recv()

    @planes(0, 16)
    def _(x):
        value = ws1[x] * f1p[x]
        wf1[x] = value
        u1a[x] = value

    sweeps(u1a, u1b, wf1, ws1, 0.25, 1, 15, False)
    u1b[0] = jnp.zeros((24, 128), jnp.float32)
    u1b[15] = jnp.zeros((24, 128), jnp.float32)

    @planes(0, 4, 1)
    def _(x):
        parts = []
        for k in range(2):
            at = 4 + 2 * x + k
            c, total = plane_neighbours(u1b, at, False)
            parts.append(f1p[at] - (1.5 + screen_weight * rho1p[at]) * c + 0.25 * total)
        rt1[x] = parts[0] + parts[1]

    gsend[0:4] = pool_to_2(rt1[:, 8:16])
    mine = sb * ns + sp

    def tell(k, carry):
        peer = lax.rem(me + k, n)
        pltpu.make_async_remote_copy(
            src_ref=gsend,
            dst_ref=gath.at[mine],
            send_sem=gsend_sem,
            recv_sem=grecv_sem,
            device_id=(peer // nb, lax.rem(peer, nb)),
            device_id_type=MESH,
        ).start()
        return carry

    lax.fori_loop(1, n, tell, 0)
    gath[mine] = gsend[...]
    u2p[...] = jnp.zeros_like(u2p)
    every = gath.at[pl.ds(0, n - 1)]
    pltpu.make_async_copy(every, every, grecv_sem).wait()
    x2, x3 = ns * 4, ns * 2
    rows2, rows3 = nb * x2, nb * x3
    for b in range(nb):
        for s in range(ns):
            f2g[b, 4 * s : 4 * s + 4] = gath[b * ns + s, 0:4]
            rho2g[b, 4 * s : 4 * s + 4] = gath[b * ns + s, 4:8]
    f2 = f2g[...].reshape(rows2, 128)
    rho2 = rho2g[...].reshape(rows2, 128)
    diag2 = 0.375 + screen_weight * rho2
    w2 = relax_weight / diag2
    r3, r2 = grid_iota((rows3, rows2))
    pool_rows = one_where(r2 // 2 == r3)
    t2, t3 = grid_iota((rows2, rows3))
    grow_rows = one_where(t2 // 2 == t3)
    pool_l = one_where((zr // 64) * 16 + (zr % 32) // 2 == zc, 0.125)
    grow_l = one_where((zc // 64) * 16 + (zc % 32) // 2 == zr)
    rho3 = dot(dot(pool_rows, rho2), pool_l)
    lane3 = grid_iota((rows3, 128))[1]
    w3 = jnp.where(lane3 < 32, relax_weight / (0.09375 + screen_weight * rho3), 0.0)

    def step2(u):
        total = flat_neighbours(u, x2, 32, 4)
        return (1.0 - relax_weight) * u + w2 * (f2 + 0.0625 * total)

    u2 = step2(w2 * f2)
    res2 = f2 - diag2 * u2 + 0.0625 * flat_neighbours(u2, x2, 32, 4)
    f3 = dot(dot(pool_rows, res2), pool_l)
    u3 = w3 * f3
    for _ in range(COARSE - 1):
        total = flat_neighbours(u3, x3, 16, 2)
        u3 = (1.0 - relax_weight) * u3 + w3 * (f3 + 0.015625 * total)
    u2 = u2 + dot(grow_rows, dot(u3, grow_l))
    u2 = step2(step2(u2))
    u2p[1 : nb + 1, 8 : 8 + x2] = u2.reshape(nb, x2, 128)

    near = [u2p[sb + o, pl.ds(4 * sp + 6, 8), :] for o in range(3)]
    q0, q1 = grid_iota((128, 512))
    grow_q = one_where(
        jnp.logical_and(q0 // 32 == q1 // 128, jnp.logical_and(q0 % 32 == (q1 % 128) // 2, q1 % 128 < 64))
    )
    fan = dot(jnp.concatenate(near, axis=0), grow_q)
    order = [(0, 2), (0, 3), (1, 0), (1, 1), (1, 2), (1, 3), (2, 0), (2, 1)]
    for at, (o, j) in enumerate(order):
        c2[:, at, :] = fan[8 * o : 8 * o + 8, 128 * j : 128 * j + 128]
    for i in range(8):
        for k in range(2):
            for m in range(2):
                rows = pl.ds(4 + m, 8, stride=2)
                u1b[2 * i + k, rows, :] = u1b[2 * i + k, rows, :] + c2[i]
    sweeps(u1b, u1a, wf1, ws1, 0.25, 2, 14, False)
    sweeps(u1a, u1b, wf1, ws1, 0.25, 3, 13, False)
    grow_z = one_where(zr == zc // 2)
    pr[...] = dot(u1b[3:13].reshape(240, 128), grow_z).reshape(10, 24, 128)

    @planes(0, 10, 1)
    def _(i):
        for k in range(2):
            for m in range(2):
                rows = pl.ds(m, 16, stride=2)
                ub[2 * i + 2 + k, rows, :] = ub[2 * i + 2 + k, rows, :] + pr[i, 4:20]

    sweeps(ub, ua, wf, ws, 1.0, 3, 21, True)

    @planes(4, 20)
    def _(x):
        c, total = plane_neighbours(ua, x, True)
        full = (1.0 - relax_weight) * c + (wf[x] + ws[x] * total)
        out[x - 4] = full[8:24]

    for halo in (rho_halo, f_halo, rho1_halo, f1_halo):
        halo.wait_send()
    for dx, dy, copy in faces:
        pl.when(has(dx, dy))(copy.wait_send)
    pltpu.make_async_copy(every, every, gsend_sem).wait()


def cycle(grid):
    ns, nb = lax.axis_size("space"), lax.axis_size("sub")
    n = ns * nb
    vm = lambda *shape: pltpu.VMEM(shape, jnp.float32)
    fine, mid = (24, 32, 128), (16, 24, 128)
    return pl.pallas_call(
        functools.partial(cycle_kernel, ns, nb),
        out_shape=jax.ShapeDtypeStruct((CX, CY, CZ), jnp.float32),
        in_specs=[pl.BlockSpec(memory_space=pltpu.VMEM)],
        out_specs=pl.BlockSpec(memory_space=pltpu.VMEM),
        scratch_shapes=[
            vm(18, 16, 128), vm(16, 32, 128), vm(*fine), vm(*fine), vm(*fine), vm(*fine),
            vm(*fine), vm(*fine), vm(8, 32, 128),
            vm(*mid), vm(*mid), vm(*mid), vm(*mid), vm(*mid), vm(*mid), vm(4, 24, 128),
            vm(10, 24, 128),
            vm(8, 128), vm(n, 8, 128), vm(nb, ns * 4, 128), vm(nb, ns * 4, 128),
            vm(nb + 2, ns * 4 + 16, 128), vm(8, 8, 128),
            pltpu.SemaphoreType.DMA((36,)),
            pltpu.SemaphoreType.DMA((36,)),
            pltpu.SemaphoreType.DMA,
            pltpu.SemaphoreType.DMA,
        ],
        compiler_params=pltpu.CompilerParams(
            collective_id=0, has_side_effects=True, vmem_limit_bytes=48 * 1024 * 1024
        ),
        name="cycle",
    )(grid)


def on_device(offsets, normals, density, tile_brick, tile_count):
    space_count = lax.axis_size("space")
    sub_count = lax.axis_size("sub")
    tiles_each = offsets.shape[4]
    slot_total = offsets.shape[6]
    brick_total = CX // BRICK * (CY // BRICK) * (CZ // BRICK)
    offsets_local = offsets.reshape(space_count, sub_count, tiles_each, 3, slot_total)
    samples = jnp.concatenate(
        [
            normals.reshape(space_count, sub_count, tiles_each, 3, slot_total),
            density.reshape(space_count, sub_count, tiles_each, 1, slot_total),
        ],
        axis=3,
    )
    slot_numbers = lax.broadcasted_iota(
        jnp.int32, (space_count, sub_count, tiles_each, slot_total), 3
    )
    live_slots = (
        slot_numbers < tile_count.reshape(space_count, sub_count, tiles_each)[..., None]
    ).astype(jnp.float32)
    samples = samples * live_slots[:, :, :, None, :]
    brick_ids = tile_brick.reshape(space_count, sub_count, tiles_each).astype(jnp.float32)
    partials_out = splat_blocks(
        offsets_local.reshape(-1, 3, slot_total), samples.reshape(-1, 4, slot_total)
    )
    partials_out = partials_out.reshape(space_count, sub_count, tiles_each, -1)
    partials_in, brick_in = (
        lax.all_to_all(
            lax.all_to_all(partials_out, "space", split_axis=0, concat_axis=0, tiled=True),
            "sub",
            split_axis=1,
            concat_axis=1,
            tiled=True,
        ),
        lax.all_to_all(
            lax.all_to_all(brick_ids, "space", split_axis=0, concat_axis=0, tiled=True),
            "sub",
            split_axis=1,
            concat_axis=1,
            tiled=True,
        ),
    )
    partials = partials_in.reshape(space_count * sub_count * tiles_each, -1)
    brick_numbers = jnp.arange(brick_total, dtype=jnp.float32)
    onehot = (brick_in.reshape(-1)[None, :] == brick_numbers[:, None]).astype(jnp.float32)
    sums = jnp.dot(
        onehot, partials, precision=lax.Precision.HIGHEST, preferred_element_type=jnp.float32
    )
    grid = to_grid(sums)
    density_field = grid[3]
    indicator = cycle(grid)
    return (indicator, density_field)


def solution(mesh):
    placed = (
        P("space", "sub", None, None, None, None, None),
        P("space", "sub", None, None, None, None, None),
        P("space", "sub", None, None, None, None),
        P("space", "sub", None, None, None),
        P("space", "sub", None, None, None),
    )
    return jax.shard_map(
        on_device,
        mesh=mesh,
        in_specs=placed,
        out_specs=(P("space", "sub", None), P("space", "sub", None)),
        check_vma=False,
    )
```

```python
import functools

import jax
import jax.numpy as jnp
from jax import lax
from jax.experimental import pallas as pl
from jax.experimental.pallas import tpu as pltpu
from jax.sharding import PartitionSpec as P

BRICK = 8
CX = 16
CY = 16
CZ = 128
LEVELS = 4
SWEEPS = 2
COARSE = 8


screen_weight = 0.05
relax_weight = 0.8


HX = 4
HY = 8
MESH = pl.DeviceIdType.MESH
HIGHEST = lax.Precision.HIGHEST


def dot(a, b):
    return jnp.dot(a, b, precision=HIGHEST, preferred_element_type=jnp.float32)


def grid_iota(shape):
    return lax.broadcasted_iota(jnp.int32, shape, 0), lax.broadcasted_iota(jnp.int32, shape, 1)


def one_where(mask, value=1.0):
    return jnp.where(mask, jnp.float32(value), jnp.float32(0.0))


def shifted_z(c, zero_ends):
    zp = pltpu.roll(c, 127, c.ndim - 1)
    zm = pltpu.roll(c, 1, c.ndim - 1)
    if zero_ends:
        lane = lax.broadcasted_iota(jnp.int32, c.shape, c.ndim - 1)
        zp = jnp.where(lane < 127, zp, 0.0)
        zm = jnp.where(lane > 0, zm, 0.0)
    return zp + zm


def plane_neighbours(ref, x, zero_ends):
    c = ref[x]
    rows = c.shape[0]
    total = ref[x - 1] + ref[x + 1]
    total = total + pltpu.roll(c, 1, 0) + pltpu.roll(c, rows - 1, 0)
    return c, total + shifted_z(c, zero_ends)


def flat_neighbours(u, xs, zl, yl):
    row, lane = grid_iota(u.shape)
    rows = u.shape[0]
    xi, zi, yi = row % xs, lane % zl, lane // zl
    total = jnp.where(zi < zl - 1, pltpu.roll(u, 127, 1), 0.0)
    total = total + jnp.where(zi > 0, pltpu.roll(u, 1, 1), 0.0)
    total = total + jnp.where(xi < xs - 1, pltpu.roll(u, rows - 1, 0), 0.0)
    total = total + jnp.where(xi > 0, pltpu.roll(u, 1, 0), 0.0)
    far_up = pltpu.roll(pltpu.roll(u, zl * (yl - 1), 1), rows - xs, 0)
    far_up = jnp.where(row < rows - xs, far_up, 0.0)
    total = total + jnp.where(yi < yl - 1, pltpu.roll(u, 128 - zl, 1), far_up)
    far_down = pltpu.roll(pltpu.roll(u, 128 - zl * (yl - 1), 1), xs, 0)
    far_down = jnp.where(row >= xs, far_down, 0.0)
    return total + jnp.where(yi > 0, pltpu.roll(u, zl, 1), far_down)


class Halo:
    def __init__(self, ref, nx, ny, send, recv, base, has, place):
        self.ref, self.nx, self.ny = ref, nx, ny
        self.has = has
        self.items = []
        k = base
        for dx in (-1, 0, 1):
            for dy in (-1, 0, 1):
                if dx == 0 and dy == 0:
                    continue
                sx = {1: (nx, HX), -1: (HX, HX), 0: (HX, nx)}[dx]
                tx = {1: (0, HX), -1: (HX + nx, HX), 0: (HX, nx)}[dx]
                sy = {1: (ny, HY), -1: (HY, HY), 0: (HY, ny)}[dy]
                ty = {1: (0, HY), -1: (HY + ny, HY), 0: (HY, ny)}[dy]
                copy = pltpu.make_async_remote_copy(
                    src_ref=ref.at[pl.ds(*sx), pl.ds(*sy)],
                    dst_ref=ref.at[pl.ds(*tx), pl.ds(*ty)],
                    send_sem=send.at[k],
                    recv_sem=recv.at[k],
                    device_id=place(dx, dy),
                    device_id_type=MESH,
                )
                self.items.append((dx, dy, copy))
                k += 1

    def clear_rim(self):
        ref, nx, ny = self.ref, self.nx, self.ny

        @pl.when(jnp.logical_not(self.has(-1, 0)))
        def _():
            ref[0:HX] = jnp.zeros((HX,) + ref.shape[1:], jnp.float32)

        @pl.when(jnp.logical_not(self.has(1, 0)))
        def _():
            ref[HX + nx :] = jnp.zeros((HX,) + ref.shape[1:], jnp.float32)

        @pl.when(jnp.logical_not(self.has(0, -1)))
        def _():
            ref[:, 0:HY] = jnp.zeros((ref.shape[0], HY, 128), jnp.float32)

        @pl.when(jnp.logical_not(self.has(0, 1)))
        def _():
            ref[:, HY + ny :] = jnp.zeros((ref.shape[0], HY, 128), jnp.float32)

    def start(self):
        for dx, dy, copy in self.items:
            pl.when(self.has(dx, dy))(copy.start)

    def wait_recv(self):
        for dx, dy, copy in self.items:
            pl.when(self.has(-dx, -dy))(copy.wait_recv)

    def wait_send(self):
        for dx, dy, copy in self.items:
            pl.when(self.has(dx, dy))(copy.wait_send)


def planes(start, stop, unroll=2):
    def wrap(body):
        def step(x, carry):
            body(x)
            return carry

        lax.fori_loop(start, stop, step, 0, unroll=unroll)

    return wrap


def cycle_kernel(
    ns, nb, g, out,
    vxp, vyp, rhop, fp, ua, ub, wf, ws, rt,
    rho1p, f1p, u1a, u1b, wf1, ws1, rt1, pr,
    gsend, gath, f2g, rho2g, u2p, c2,
    send, recv, gsend_sem, grecv_sem,
):
    n = ns * nb
    sp, sb = lax.axis_index("space"), lax.axis_index("sub")
    me = sp * nb + sb

    def place(dx, dy):
        return (lax.rem(sp + dx + ns, ns), lax.rem(sb + dy + nb, nb))

    def has(dx, dy):
        ok = jnp.bool_(True)
        if dx:
            ok = sp + dx >= 0 if dx < 0 else sp + dx < ns
        if dy:
            oky = sb + dy >= 0 if dy < 0 else sb + dy < nb
            ok = jnp.logical_and(ok, oky) if dx else oky
        return ok

    barrier = pltpu.get_barrier_semaphore()

    def greet(k, carry):
        peer = lax.rem(me + k, n)
        pl.semaphore_signal(
            barrier, inc=1, device_id=(peer // nb, lax.rem(peer, nb)), device_id_type=MESH
        )
        return carry

    lax.fori_loop(1, n, greet, 0)

    rho_halo = Halo(rhop, 16, 16, send, recv, 0, has, place)
    f_halo = Halo(fp, 16, 16, send, recv, 8, has, place)
    rho1_halo = Halo(rho1p, 8, 8, send, recv, 16, has, place)
    f1_halo = Halo(f1p, 8, 8, send, recv, 24, has, place)

    def face(src, dst, k, dx, dy):
        return (
            dx,
            dy,
            pltpu.make_async_remote_copy(
                src_ref=src,
                dst_ref=dst,
                send_sem=send.at[k],
                recv_sem=recv.at[k],
                device_id=place(dx, dy),
                device_id_type=MESH,
            ),
        )

    faces = [
        face(vxp.at[16], vxp.at[0], 32, 1, 0),
        face(vxp.at[1], vxp.at[17], 33, -1, 0),
        face(vyp.at[:, pl.ds(16, 8)], vyp.at[:, pl.ds(0, 8)], 34, 0, 1),
        face(vyp.at[:, pl.ds(8, 8)], vyp.at[:, pl.ds(24, 8)], 35, 0, -1),
    ]
    vxp[1:17] = g[0]
    vyp[:, 8:24] = g[1]
    rhop[4:20, 8:24] = g[3]
    for halo in (rho_halo, f_halo, rho1_halo, f1_halo):
        halo.clear_rim()

    @pl.when(jnp.logical_not(has(-1, 0)))
    def _():
        vxp[0] = jnp.zeros((16, 128), jnp.float32)

    @pl.when(jnp.logical_not(has(1, 0)))
    def _():
        vxp[17] = jnp.zeros((16, 128), jnp.float32)

    @pl.when(jnp.logical_not(has(0, -1)))
    def _():
        vyp[:, 0:8] = jnp.zeros((16, 8, 128), jnp.float32)

    @pl.when(jnp.logical_not(has(0, 1)))
    def _():
        vyp[:, 24:32] = jnp.zeros((16, 8, 128), jnp.float32)

    zr, zc = grid_iota((128, 128))
    pool_z = one_where(zr // 2 == zc, 0.125)

    def pool_to_1(dst):
        pooled = rt[:, pl.ds(8, 8, stride=2), :] + rt[:, pl.ds(9, 8, stride=2), :]
        dst[4:12, 8:16] = dot(pooled.reshape(64, 128), pool_z).reshape(8, 8, 128)

    pool_lanes = one_where(zr // 2 == zc % 32, 0.125)
    prow = lax.broadcasted_iota(jnp.int32, (4, 8, 128), 1)
    plane_lane = lax.broadcasted_iota(jnp.int32, (4, 8, 128), 2)
    pick_rows = plane_lane // 32 == prow // 2

    def pool_to_2(value):
        spread = dot(value.reshape(32, 128), pool_lanes).reshape(4, 8, 128)
        return jnp.sum(jnp.where(pick_rows, spread, 0.0), axis=1)

    pl.semaphore_wait(barrier, n - 1)
    for dx, dy, copy in faces:
        pl.when(has(dx, dy))(copy.start)
    rho_halo.start()

    @planes(0, 8)
    def _(x):
        rt[x, 8:24] = g[3, 2 * x] + g[3, 2 * x + 1]

    pool_to_1(rho1p)
    rho1_halo.start()
    for i in range(4):
        rt1[i, 8:16] = rho1p[4 + 2 * i, 8:16] + rho1p[5 + 2 * i, 8:16]
    gsend[4:8] = pool_to_2(rt1[:, 8:16])

    for dx, dy, copy in faces:
        pl.when(has(-dx, -dy))(copy.wait_recv)

    lane16 = lax.broadcasted_iota(jnp.int32, (16, 128), 1)

    @planes(0, 16)
    def _(x):
        change = vxp[x + 2] - vxp[x]
        change = change + (vyp[x, 9:25] - vyp[x, 7:23])
        vz = g[2, x]
        zp = jnp.where(lane16 < 127, pltpu.roll(vz, 127, 1), 0.0)
        zm = jnp.where(lane16 > 0, pltpu.roll(vz, 1, 1), 0.0)
        fp[x + 4, 8:24] = -0.5 * (change + (zp - zm))

    f_halo.start()
    rho_halo.wait_recv()

    def inside(x, rows, lanes, step):
        r, l = grid_iota((rows, 128))
        gx = sp * step + x - HX
        gy = sb * step + r - HY
        ok = jnp.logical_and(gy >= 0, gy < nb * step)
        ok = jnp.logical_and(ok, jnp.logical_and(gx >= 0, gx < ns * step))
        return jnp.logical_and(ok, l < lanes) if lanes < 128 else ok

    @planes(0, 24)
    def _(x):
        ws[x] = jnp.where(inside(x, 32, 128, 16), relax_weight / (6.0 + screen_weight * rhop[x]), 0.0)

    rho1_halo.wait_recv()

    @planes(0, 16)
    def _(x):
        ws1[x] = jnp.where(
            inside(x, 24, 64, 8), relax_weight / (1.5 + screen_weight * rho1p[x]), 0.0
        )

    f_halo.wait_recv()

    @planes(1, 23)
    def _(x):
        value = ws[x] * fp[x]
        wf[x] = value
        ua[x] = value

    def sweeps(src, dst, wf_ref, ws_ref, scale, start, stop, zero_ends):
        @planes(start, stop)
        def _(x):
            c, total = plane_neighbours(src, x, zero_ends)
            if scale != 1.0:
                total = scale * total
            dst[x] = (1.0 - relax_weight) * c + (wf_ref[x] + ws_ref[x] * total)

    sweeps(ua, ub, wf, ws, 1.0, 2, 22, True)

    @planes(0, 8, 1)
    def _(x):
        parts = []
        for k in range(2):
            at = 4 + 2 * x + k
            c, total = plane_neighbours(ub, at, True)
            parts.append(fp[at] - (6.0 + screen_weight * rhop[at]) * c + total)
        rt[x] = parts[0] + parts[1]

    pool_to_1(f1p)
    f1_halo.start()
    f1_halo.wait_recv()

    @planes(0, 16)
    def _(x):
        value = ws1[x] * f1p[x]
        wf1[x] = value
        u1a[x] = value

    sweeps(u1a, u1b, wf1, ws1, 0.25, 1, 15, False)
    u1b[0] = jnp.zeros((24, 128), jnp.float32)
    u1b[15] = jnp.zeros((24, 128), jnp.float32)

    @planes(0, 4, 1)
    def _(x):
        parts = []
        for k in range(2):
            at = 4 + 2 * x + k
            c, total = plane_neighbours(u1b, at, False)
            parts.append(f1p[at] - (1.5 + screen_weight * rho1p[at]) * c + 0.25 * total)
        rt1[x] = parts[0] + parts[1]

    gsend[0:4] = pool_to_2(rt1[:, 8:16])
    mine = sb * ns + sp

    def tell(k, carry):
        peer = lax.rem(me + k, n)
        pltpu.make_async_remote_copy(
            src_ref=gsend,
            dst_ref=gath.at[mine],
            send_sem=gsend_sem,
            recv_sem=grecv_sem,
            device_id=(peer // nb, lax.rem(peer, nb)),
            device_id_type=MESH,
        ).start()
        return carry

    lax.fori_loop(1, n, tell, 0)
    gath[mine] = gsend[...]
    u2p[...] = jnp.zeros_like(u2p)
    every = gath.at[pl.ds(0, n - 1)]
    pltpu.make_async_copy(every, every, grecv_sem).wait()
    x2, x3 = ns * 4, ns * 2
    rows2, rows3 = nb * x2, nb * x3
    for b in range(nb):
        for s in range(ns):
            f2g[b, 4 * s : 4 * s + 4] = gath[b * ns + s, 0:4]
            rho2g[b, 4 * s : 4 * s + 4] = gath[b * ns + s, 4:8]
    f2 = f2g[...].reshape(rows2, 128)
    rho2 = rho2g[...].reshape(rows2, 128)
    diag2 = 0.375 + screen_weight * rho2
    w2 = relax_weight / diag2
    r3, r2 = grid_iota((rows3, rows2))
    pool_rows = one_where(r2 // 2 == r3)
    t2, t3 = grid_iota((rows2, rows3))
    grow_rows = one_where(t2 // 2 == t3)
    pool_l = one_where((zr // 64) * 16 + (zr % 32) // 2 == zc, 0.125)
    grow_l = one_where((zc // 64) * 16 + (zc % 32) // 2 == zr)
    rho3 = dot(dot(pool_rows, rho2), pool_l)
    lane3 = grid_iota((rows3, 128))[1]
    w3 = jnp.where(lane3 < 32, relax_weight / (0.09375 + screen_weight * rho3), 0.0)

    def step2(u):
        total = flat_neighbours(u, x2, 32, 4)
        return (1.0 - relax_weight) * u + w2 * (f2 + 0.0625 * total)

    u2 = step2(w2 * f2)
    res2 = f2 - diag2 * u2 + 0.0625 * flat_neighbours(u2, x2, 32, 4)
    f3 = dot(dot(pool_rows, res2), pool_l)
    u3 = w3 * f3
    for _ in range(COARSE - 1):
        total = flat_neighbours(u3, x3, 16, 2)
        u3 = (1.0 - relax_weight) * u3 + w3 * (f3 + 0.015625 * total)
    u2 = u2 + dot(grow_rows, dot(u3, grow_l))
    u2 = step2(step2(u2))
    u2p[1 : nb + 1, 8 : 8 + x2] = u2.reshape(nb, x2, 128)

    near = [u2p[sb + o, pl.ds(4 * sp + 6, 8), :] for o in range(3)]
    q0, q1 = grid_iota((128, 512))
    grow_q = one_where(
        jnp.logical_and(q0 // 32 == q1 // 128, jnp.logical_and(q0 % 32 == (q1 % 128) // 2, q1 % 128 < 64))
    )
    fan = dot(jnp.concatenate(near, axis=0), grow_q)
    order = [(0, 2), (0, 3), (1, 0), (1, 1), (1, 2), (1, 3), (2, 0), (2, 1)]
    for at, (o, j) in enumerate(order):
        c2[:, at, :] = fan[8 * o : 8 * o + 8, 128 * j : 128 * j + 128]
    for i in range(8):
        for k in range(2):
            for m in range(2):
                rows = pl.ds(4 + m, 8, stride=2)
                u1b[2 * i + k, rows, :] = u1b[2 * i + k, rows, :] + c2[i]
    sweeps(u1b, u1a, wf1, ws1, 0.25, 2, 14, False)
    sweeps(u1a, u1b, wf1, ws1, 0.25, 3, 13, False)
    grow_z = one_where(zr == zc // 2)
    pr[...] = dot(u1b[3:13].reshape(240, 128), grow_z).reshape(10, 24, 128)

    @planes(0, 10, 1)
    def _(i):
        for k in range(2):
            for m in range(2):
                rows = pl.ds(m, 16, stride=2)
                ub[2 * i + 2 + k, rows, :] = ub[2 * i + 2 + k, rows, :] + pr[i, 4:20]

    sweeps(ub, ua, wf, ws, 1.0, 3, 21, True)

    @planes(4, 20)
    def _(x):
        c, total = plane_neighbours(ua, x, True)
        full = (1.0 - relax_weight) * c + (wf[x] + ws[x] * total)
        out[x - 4] = full[8:24]

    for halo in (rho_halo, f_halo, rho1_halo, f1_halo):
        halo.wait_send()
    for dx, dy, copy in faces:
        pl.when(has(dx, dy))(copy.wait_send)
    pltpu.make_async_copy(every, every, gsend_sem).wait()


def cycle(grid):
    ns, nb = lax.axis_size("space"), lax.axis_size("sub")
    n = ns * nb
    vm = lambda *shape: pltpu.VMEM(shape, jnp.float32)
    fine, mid = (24, 32, 128), (16, 24, 128)
    return pl.pallas_call(
        functools.partial(cycle_kernel, ns, nb),
        out_shape=jax.ShapeDtypeStruct((CX, CY, CZ), jnp.float32),
        in_specs=[pl.BlockSpec(memory_space=pltpu.VMEM)],
        out_specs=pl.BlockSpec(memory_space=pltpu.VMEM),
        scratch_shapes=[
            vm(18, 16, 128), vm(16, 32, 128), vm(*fine), vm(*fine), vm(*fine), vm(*fine),
            vm(*fine), vm(*fine), vm(8, 32, 128),
            vm(*mid), vm(*mid), vm(*mid), vm(*mid), vm(*mid), vm(*mid), vm(4, 24, 128),
            vm(10, 24, 128),
            vm(8, 128), vm(n, 8, 128), vm(nb, ns * 4, 128), vm(nb, ns * 4, 128),
            vm(nb + 2, ns * 4 + 16, 128), vm(8, 8, 128),
            pltpu.SemaphoreType.DMA((36,)),
            pltpu.SemaphoreType.DMA((36,)),
            pltpu.SemaphoreType.DMA,
            pltpu.SemaphoreType.DMA,
        ],
        compiler_params=pltpu.CompilerParams(
            collective_id=0, has_side_effects=True, vmem_limit_bytes=48 * 1024 * 1024
        ),
        name="cycle",
    )(grid)


def exchange_kernel(ns, nb, src, dst, send_sem, recv_sem, own_sem):
    n = ns * nb
    me = lax.axis_index("space") * nb + lax.axis_index("sub")
    barrier = pltpu.get_barrier_semaphore()

    def where(k):
        peer = lax.rem(me + k, n)
        return peer, (peer // nb, lax.rem(peer, nb))

    def greet(k, carry):
        pl.semaphore_signal(barrier, inc=1, device_id=where(k)[1], device_id_type=MESH)
        return carry

    lax.fori_loop(1, n, greet, 0)
    own = pltpu.make_async_copy(src.at[me], dst.at[me], own_sem)
    own.start()
    pl.semaphore_wait(barrier, n - 1)

    def tell(k, carry):
        peer, place = where(k)
        pltpu.make_async_remote_copy(
            src_ref=src.at[peer],
            dst_ref=dst.at[me],
            send_sem=send_sem,
            recv_sem=recv_sem,
            device_id=place,
            device_id_type=MESH,
        ).start()
        return carry

    lax.fori_loop(1, n, tell, 0)
    own.wait()
    every = dst.at[pl.ds(0, n - 1)]
    pltpu.make_async_copy(every, every, recv_sem).wait()
    pltpu.make_async_copy(every, every, send_sem).wait()


def exchange(packed):
    ns, nb = lax.axis_size("space"), lax.axis_size("sub")
    return pl.pallas_call(
        functools.partial(exchange_kernel, ns, nb),
        out_shape=jax.ShapeDtypeStruct(packed.shape, jnp.float32),
        in_specs=[pl.BlockSpec(memory_space=pl.ANY)],
        out_specs=pl.BlockSpec(memory_space=pl.ANY),
        scratch_shapes=[pltpu.SemaphoreType.DMA] * 3,
        compiler_params=pltpu.CompilerParams(collective_id=1, has_side_effects=True),
        name="exchange",
    )(packed)


def splat_kernel(ids, points, grid, acc):
    peers, tiles = points.shape[0], points.shape[1]
    acc[...] = jnp.zeros_like(acc)
    centers = lax.broadcasted_iota(jnp.int32, (BRICK, 128), 0).astype(jnp.float32) + 0.5

    def split(value):
        high = value.astype(jnp.bfloat16)
        low = (value - high.astype(jnp.float32)).astype(jnp.bfloat16)
        return jnp.concatenate([high, low], axis=0)

    def one_tile(p, t):
        rows = points[p, t]
        wx, wy, wz = (
            jnp.maximum(0.0, 1.0 - jnp.abs(rows[d : d + 1] - centers)) for d in range(3)
        )
        planar = jnp.concatenate([wx[i : i + 1] * wy for i in range(BRICK)], axis=0)
        loaded = jnp.concatenate([rows[3 + c : 4 + c] * wz for c in range(4)], axis=0)
        full = lax.dot_general(
            split(planar),
            split(loaded),
            (((1,), (1,)), ((), ())),
            preferred_element_type=jnp.float32,
        )
        return full[0:64] + full[64:128]

    def one_peer(p, carry):
        parts = [one_tile(p, t) for t in range(tiles)]
        for t in range(tiles):
            brick = ids[p * tiles + t]
            acc[brick, :, 0:64] = acc[brick, :, 0:64] + parts[t]
        return carry

    lax.fori_loop(0, peers, one_peer, 0, unroll=2)

    group = lax.broadcasted_iota(jnp.int32, (BRICK, 128), 1) // BRICK
    nz = CZ // BRICK

    for column in range(acc.shape[0] // nz):
        bx, by = column // (CY // BRICK), column % (CY // BRICK)

        def one_row(i, carry):
            turned = []
            for bz in range(nz):
                part = acc[column * nz + bz, pl.ds(pl.multiple_of(8 * i, 8), 8), :]
                part = part + pltpu.roll(part, 96, 1)
                turned.append(pltpu.roll(part, 8 * bz, 1) if bz else part)
            for c in range(4):
                value = turned[0]
                for bz in range(1, nz):
                    value = jnp.where(group == (bz + c) % nz, turned[bz], value)
                if c:
                    value = pltpu.roll(value, 128 - 8 * c, 1)
                grid[c, BRICK * bx + i, BRICK * by : BRICK * by + BRICK, :] = value
            return carry

        lax.fori_loop(0, BRICK, one_row, 0, unroll=2)


def splat(ids, points):
    bricks = CX // BRICK * (CY // BRICK) * (CZ // BRICK)
    return pl.pallas_call(
        splat_kernel,
        out_shape=jax.ShapeDtypeStruct((4, CX, CY, CZ), jnp.float32),
        in_specs=[
            pl.BlockSpec(memory_space=pltpu.SMEM),
            pl.BlockSpec(memory_space=pltpu.VMEM),
        ],
        out_specs=pl.BlockSpec(memory_space=pltpu.VMEM),
        scratch_shapes=[pltpu.VMEM((bricks, 64, 128), jnp.float32)],
        compiler_params=pltpu.CompilerParams(vmem_limit_bytes=48 * 1024 * 1024),
        name="splat",
    )(ids, points)


def on_device(offsets, normals, density, tile_brick, tile_count):
    devices = lax.axis_size("space") * lax.axis_size("sub")
    tiles, slots = offsets.shape[4], offsets.shape[6]
    live = lax.broadcasted_iota(jnp.int32, (devices, tiles, 1, slots), 3) < tile_count.reshape(
        devices, tiles, 1, 1
    )
    ids = jnp.broadcast_to(
        tile_brick.reshape(devices, tiles, 1, 1).astype(jnp.float32), (devices, tiles, 1, slots)
    )
    packed = jnp.concatenate(
        [
            offsets.reshape(devices, tiles, 3, slots),
            jnp.where(live, normals.reshape(devices, tiles, 3, slots), 0.0),
            jnp.where(live, density.reshape(devices, tiles, 1, slots), 0.0),
            ids,
        ],
        axis=2,
    )
    points = exchange(packed)
    bricks = points[:, :, 7, 0].astype(jnp.int32).reshape(-1)
    grid = splat(bricks, points)
    return (cycle(grid), grid[3])


def solution(mesh):
    placed = (
        P("space", "sub", None, None, None, None, None),
        P("space", "sub", None, None, None, None, None),
        P("space", "sub", None, None, None, None),
        P("space", "sub", None, None, None),
        P("space", "sub", None, None, None),
    )
    return jax.shard_map(
        on_device,
        mesh=mesh,
        in_specs=placed,
        out_specs=(P("space", "sub", None), P("space", "sub", None)),
        check_vma=False,
    )
```

```python
import functools

import jax
import jax.numpy as jnp
from jax import lax
from jax.experimental import pallas as pl
from jax.experimental.pallas import tpu as pltpu
from jax.sharding import PartitionSpec as P

BRICK = 8
CX = 16
CY = 16
CZ = 128
LEVELS = 4
SWEEPS = 2
COARSE = 8


screen_weight = 0.05
relax_weight = 0.8


HX = 4
HY = 8
MESH = pl.DeviceIdType.MESH
HIGHEST = lax.Precision.HIGHEST


def dot(a, b):
    return jnp.dot(a, b, precision=HIGHEST, preferred_element_type=jnp.float32)


def grid_iota(shape):
    return lax.broadcasted_iota(jnp.int32, shape, 0), lax.broadcasted_iota(jnp.int32, shape, 1)


def one_where(mask, value=1.0):
    return jnp.where(mask, jnp.float32(value), jnp.float32(0.0))


def shifted_z(c, zero_ends):
    zp = pltpu.roll(c, 127, c.ndim - 1)
    zm = pltpu.roll(c, 1, c.ndim - 1)
    if zero_ends:
        lane = lax.broadcasted_iota(jnp.int32, c.shape, c.ndim - 1)
        zp = jnp.where(lane < 127, zp, 0.0)
        zm = jnp.where(lane > 0, zm, 0.0)
    return zp + zm


def plane_neighbours(ref, x, zero_ends):
    c = ref[x]
    rows = c.shape[0]
    total = ref[x - 1] + ref[x + 1]
    total = total + pltpu.roll(c, 1, 0) + pltpu.roll(c, rows - 1, 0)
    return c, total + shifted_z(c, zero_ends)


def flat_neighbours(u, xs, zl, yl):
    row, lane = grid_iota(u.shape)
    rows = u.shape[0]
    xi, zi, yi = row % xs, lane % zl, lane // zl
    total = jnp.where(zi < zl - 1, pltpu.roll(u, 127, 1), 0.0)
    total = total + jnp.where(zi > 0, pltpu.roll(u, 1, 1), 0.0)
    total = total + jnp.where(xi < xs - 1, pltpu.roll(u, rows - 1, 0), 0.0)
    total = total + jnp.where(xi > 0, pltpu.roll(u, 1, 0), 0.0)
    far_up = pltpu.roll(pltpu.roll(u, zl * (yl - 1), 1), rows - xs, 0)
    far_up = jnp.where(row < rows - xs, far_up, 0.0)
    total = total + jnp.where(yi < yl - 1, pltpu.roll(u, 128 - zl, 1), far_up)
    far_down = pltpu.roll(pltpu.roll(u, 128 - zl * (yl - 1), 1), xs, 0)
    far_down = jnp.where(row >= xs, far_down, 0.0)
    return total + jnp.where(yi > 0, pltpu.roll(u, zl, 1), far_down)


class Halo:
    def __init__(self, ref, nx, ny, send, recv, base, has, place):
        self.ref, self.nx, self.ny = ref, nx, ny
        self.has = has
        self.items = []
        k = base
        for dx in (-1, 0, 1):
            for dy in (-1, 0, 1):
                if dx == 0 and dy == 0:
                    continue
                sx = {1: (nx, HX), -1: (HX, HX), 0: (HX, nx)}[dx]
                tx = {1: (0, HX), -1: (HX + nx, HX), 0: (HX, nx)}[dx]
                sy = {1: (ny, HY), -1: (HY, HY), 0: (HY, ny)}[dy]
                ty = {1: (0, HY), -1: (HY + ny, HY), 0: (HY, ny)}[dy]
                copy = pltpu.make_async_remote_copy(
                    src_ref=ref.at[pl.ds(*sx), pl.ds(*sy)],
                    dst_ref=ref.at[pl.ds(*tx), pl.ds(*ty)],
                    send_sem=send.at[k],
                    recv_sem=recv.at[k],
                    device_id=place(dx, dy),
                    device_id_type=MESH,
                )
                self.items.append((dx, dy, copy))
                k += 1

    def clear_rim(self):
        ref, nx, ny = self.ref, self.nx, self.ny

        @pl.when(jnp.logical_not(self.has(-1, 0)))
        def _():
            ref[0:HX] = jnp.zeros((HX,) + ref.shape[1:], jnp.float32)

        @pl.when(jnp.logical_not(self.has(1, 0)))
        def _():
            ref[HX + nx :] = jnp.zeros((HX,) + ref.shape[1:], jnp.float32)

        @pl.when(jnp.logical_not(self.has(0, -1)))
        def _():
            ref[:, 0:HY] = jnp.zeros((ref.shape[0], HY, 128), jnp.float32)

        @pl.when(jnp.logical_not(self.has(0, 1)))
        def _():
            ref[:, HY + ny :] = jnp.zeros((ref.shape[0], HY, 128), jnp.float32)

    def start(self):
        for dx, dy, copy in self.items:
            pl.when(self.has(dx, dy))(copy.start)

    def wait_recv(self):
        for dx, dy, copy in self.items:
            pl.when(self.has(-dx, -dy))(copy.wait_recv)

    def wait_send(self):
        for dx, dy, copy in self.items:
            pl.when(self.has(dx, dy))(copy.wait_send)


def planes(start, stop, unroll=2):
    def wrap(body):
        def step(x, carry):
            body(x)
            return carry

        lax.fori_loop(start, stop, step, 0, unroll=unroll)

    return wrap


def cycle_kernel(
    ns, nb, g, rho, out,
    vxp, vyp, rhop, fp, ua, ub, wf, ws, rt,
    rho1p, f1p, u1a, u1b, wf1, ws1, rt1, pr,
    gsend, gath, f2g, rho2g, u2p, c2,
    send, recv, gsend_sem, grecv_sem,
):
    n = ns * nb
    sp, sb = lax.axis_index("space"), lax.axis_index("sub")
    me = sp * nb + sb

    def place(dx, dy):
        return (lax.rem(sp + dx + ns, ns), lax.rem(sb + dy + nb, nb))

    def has(dx, dy):
        ok = jnp.bool_(True)
        if dx:
            ok = sp + dx >= 0 if dx < 0 else sp + dx < ns
        if dy:
            oky = sb + dy >= 0 if dy < 0 else sb + dy < nb
            ok = jnp.logical_and(ok, oky) if dx else oky
        return ok

    barrier = pltpu.get_barrier_semaphore()

    def greet(k, carry):
        peer = lax.rem(me + k, n)
        pl.semaphore_signal(
            barrier, inc=1, device_id=(peer // nb, lax.rem(peer, nb)), device_id_type=MESH
        )
        return carry

    lax.fori_loop(1, n, greet, 0)

    rho_halo = Halo(rhop, 16, 16, send, recv, 0, has, place)
    f_halo = Halo(fp, 16, 16, send, recv, 8, has, place)
    rho1_halo = Halo(rho1p, 8, 8, send, recv, 16, has, place)
    f1_halo = Halo(f1p, 8, 8, send, recv, 24, has, place)

    def face(src, dst, k, dx, dy):
        return (
            dx,
            dy,
            pltpu.make_async_remote_copy(
                src_ref=src,
                dst_ref=dst,
                send_sem=send.at[k],
                recv_sem=recv.at[k],
                device_id=place(dx, dy),
                device_id_type=MESH,
            ),
        )

    faces = [
        face(vxp.at[16], vxp.at[0], 32, 1, 0),
        face(vxp.at[1], vxp.at[17], 33, -1, 0),
        face(vyp.at[:, pl.ds(16, 8)], vyp.at[:, pl.ds(0, 8)], 34, 0, 1),
        face(vyp.at[:, pl.ds(8, 8)], vyp.at[:, pl.ds(24, 8)], 35, 0, -1),
    ]
    vxp[1:17] = g[0]
    vyp[:, 8:24] = g[1]
    rhop[4:20, 8:24] = rho[...]
    for halo in (rho_halo, f_halo, rho1_halo, f1_halo):
        halo.clear_rim()

    @pl.when(jnp.logical_not(has(-1, 0)))
    def _():
        vxp[0] = jnp.zeros((16, 128), jnp.float32)

    @pl.when(jnp.logical_not(has(1, 0)))
    def _():
        vxp[17] = jnp.zeros((16, 128), jnp.float32)

    @pl.when(jnp.logical_not(has(0, -1)))
    def _():
        vyp[:, 0:8] = jnp.zeros((16, 8, 128), jnp.float32)

    @pl.when(jnp.logical_not(has(0, 1)))
    def _():
        vyp[:, 24:32] = jnp.zeros((16, 8, 128), jnp.float32)

    zr, zc = grid_iota((128, 128))
    pool_z = one_where(zr // 2 == zc, 0.125)

    def pool_to_1(dst):
        pooled = rt[:, pl.ds(8, 8, stride=2), :] + rt[:, pl.ds(9, 8, stride=2), :]
        dst[4:12, 8:16] = dot(pooled.reshape(64, 128), pool_z).reshape(8, 8, 128)

    pool_lanes = one_where(zr // 2 == zc % 32, 0.125)
    prow = lax.broadcasted_iota(jnp.int32, (4, 8, 128), 1)
    plane_lane = lax.broadcasted_iota(jnp.int32, (4, 8, 128), 2)
    pick_rows = plane_lane // 32 == prow // 2

    def pool_to_2(value):
        spread = dot(value.reshape(32, 128), pool_lanes).reshape(4, 8, 128)
        return jnp.sum(jnp.where(pick_rows, spread, 0.0), axis=1)

    pl.semaphore_wait(barrier, n - 1)
    for dx, dy, copy in faces:
        pl.when(has(dx, dy))(copy.start)
    rho_halo.start()

    @planes(0, 8)
    def _(x):
        rt[x, 8:24] = rho[2 * x] + rho[2 * x + 1]

    pool_to_1(rho1p)
    rho1_halo.start()
    for i in range(4):
        rt1[i, 8:16] = rho1p[4 + 2 * i, 8:16] + rho1p[5 + 2 * i, 8:16]
    gsend[4:8] = pool_to_2(rt1[:, 8:16])

    for dx, dy, copy in faces:
        pl.when(has(-dx, -dy))(copy.wait_recv)

    lane16 = lax.broadcasted_iota(jnp.int32, (16, 128), 1)

    @planes(0, 16)
    def _(x):
        change = vxp[x + 2] - vxp[x]
        change = change + (vyp[x, 9:25] - vyp[x, 7:23])
        vz = g[2, x]
        zp = jnp.where(lane16 < 127, pltpu.roll(vz, 127, 1), 0.0)
        zm = jnp.where(lane16 > 0, pltpu.roll(vz, 1, 1), 0.0)
        fp[x + 4, 8:24] = -0.5 * (change + (zp - zm))

    f_halo.start()
    rho_halo.wait_recv()

    def inside(x, rows, lanes, step):
        r, l = grid_iota((rows, 128))
        gx = sp * step + x - HX
        gy = sb * step + r - HY
        ok = jnp.logical_and(gy >= 0, gy < nb * step)
        ok = jnp.logical_and(ok, jnp.logical_and(gx >= 0, gx < ns * step))
        return jnp.logical_and(ok, l < lanes) if lanes < 128 else ok

    @planes(0, 24)
    def _(x):
        ws[x] = jnp.where(inside(x, 32, 128, 16), relax_weight / (6.0 + screen_weight * rhop[x]), 0.0)

    rho1_halo.wait_recv()

    @planes(0, 16)
    def _(x):
        ws1[x] = jnp.where(
            inside(x, 24, 64, 8), relax_weight / (1.5 + screen_weight * rho1p[x]), 0.0
        )

    f_halo.wait_recv()

    @planes(1, 23)
    def _(x):
        value = ws[x] * fp[x]
        wf[x] = value
        ua[x] = value

    def sweeps(src, dst, wf_ref, ws_ref, scale, start, stop, zero_ends):
        @planes(start, stop)
        def _(x):
            c, total = plane_neighbours(src, x, zero_ends)
            if scale != 1.0:
                total = scale * total
            dst[x] = (1.0 - relax_weight) * c + (wf_ref[x] + ws_ref[x] * total)

    sweeps(ua, ub, wf, ws, 1.0, 2, 22, True)

    @planes(0, 8, 1)
    def _(x):
        parts = []
        for k in range(2):
            at = 4 + 2 * x + k
            c, total = plane_neighbours(ub, at, True)
            parts.append(fp[at] - (6.0 + screen_weight * rhop[at]) * c + total)
        rt[x] = parts[0] + parts[1]

    pool_to_1(f1p)
    f1_halo.start()
    f1_halo.wait_recv()

    @planes(0, 16)
    def _(x):
        value = ws1[x] * f1p[x]
        wf1[x] = value
        u1a[x] = value

    sweeps(u1a, u1b, wf1, ws1, 0.25, 1, 15, False)
    u1b[0] = jnp.zeros((24, 128), jnp.float32)
    u1b[15] = jnp.zeros((24, 128), jnp.float32)

    @planes(0, 4, 1)
    def _(x):
        parts = []
        for k in range(2):
            at = 4 + 2 * x + k
            c, total = plane_neighbours(u1b, at, False)
            parts.append(f1p[at] - (1.5 + screen_weight * rho1p[at]) * c + 0.25 * total)
        rt1[x] = parts[0] + parts[1]

    gsend[0:4] = pool_to_2(rt1[:, 8:16])
    mine = sb * ns + sp

    def tell(k, carry):
        peer = lax.rem(me + k, n)
        pltpu.make_async_remote_copy(
            src_ref=gsend,
            dst_ref=gath.at[mine],
            send_sem=gsend_sem,
            recv_sem=grecv_sem,
            device_id=(peer // nb, lax.rem(peer, nb)),
            device_id_type=MESH,
        ).start()
        return carry

    lax.fori_loop(1, n, tell, 0)
    gath[mine] = gsend[...]
    u2p[...] = jnp.zeros_like(u2p)
    every = gath.at[pl.ds(0, n - 1)]
    pltpu.make_async_copy(every, every, grecv_sem).wait()
    x2, x3 = ns * 4, ns * 2
    rows2, rows3 = nb * x2, nb * x3
    for b in range(nb):
        for s in range(ns):
            f2g[b, 4 * s : 4 * s + 4] = gath[b * ns + s, 0:4]
            rho2g[b, 4 * s : 4 * s + 4] = gath[b * ns + s, 4:8]
    f2 = f2g[...].reshape(rows2, 128)
    rho2 = rho2g[...].reshape(rows2, 128)
    diag2 = 0.375 + screen_weight * rho2
    w2 = relax_weight / diag2
    r3, r2 = grid_iota((rows3, rows2))
    pool_rows = one_where(r2 // 2 == r3)
    t2, t3 = grid_iota((rows2, rows3))
    grow_rows = one_where(t2 // 2 == t3)
    pool_l = one_where((zr // 64) * 16 + (zr % 32) // 2 == zc, 0.125)
    grow_l = one_where((zc // 64) * 16 + (zc % 32) // 2 == zr)
    rho3 = dot(dot(pool_rows, rho2), pool_l)
    lane3 = grid_iota((rows3, 128))[1]
    w3 = jnp.where(lane3 < 32, relax_weight / (0.09375 + screen_weight * rho3), 0.0)

    def step2(u):
        total = flat_neighbours(u, x2, 32, 4)
        return (1.0 - relax_weight) * u + w2 * (f2 + 0.0625 * total)

    u2 = step2(w2 * f2)
    res2 = f2 - diag2 * u2 + 0.0625 * flat_neighbours(u2, x2, 32, 4)
    f3 = dot(dot(pool_rows, res2), pool_l)
    u3 = w3 * f3
    for _ in range(COARSE - 1):
        total = flat_neighbours(u3, x3, 16, 2)
        u3 = (1.0 - relax_weight) * u3 + w3 * (f3 + 0.015625 * total)
    u2 = u2 + dot(grow_rows, dot(u3, grow_l))
    u2 = step2(step2(u2))
    u2p[1 : nb + 1, 8 : 8 + x2] = u2.reshape(nb, x2, 128)

    near = [u2p[sb + o, pl.ds(4 * sp + 6, 8), :] for o in range(3)]
    q0, q1 = grid_iota((128, 512))
    grow_q = one_where(
        jnp.logical_and(q0 // 32 == q1 // 128, jnp.logical_and(q0 % 32 == (q1 % 128) // 2, q1 % 128 < 64))
    )
    fan = dot(jnp.concatenate(near, axis=0), grow_q)
    order = [(0, 2), (0, 3), (1, 0), (1, 1), (1, 2), (1, 3), (2, 0), (2, 1)]
    for at, (o, j) in enumerate(order):
        c2[:, at, :] = fan[8 * o : 8 * o + 8, 128 * j : 128 * j + 128]
    for i in range(8):
        for k in range(2):
            for m in range(2):
                rows = pl.ds(4 + m, 8, stride=2)
                u1b[2 * i + k, rows, :] = u1b[2 * i + k, rows, :] + c2[i]
    sweeps(u1b, u1a, wf1, ws1, 0.25, 2, 14, False)
    sweeps(u1a, u1b, wf1, ws1, 0.25, 3, 13, False)
    grow_z = one_where(zr == zc // 2)
    pr[...] = dot(u1b[3:13].reshape(240, 128), grow_z).reshape(10, 24, 128)

    @planes(0, 10, 1)
    def _(i):
        for k in range(2):
            for m in range(2):
                rows = pl.ds(m, 16, stride=2)
                ub[2 * i + 2 + k, rows, :] = ub[2 * i + 2 + k, rows, :] + pr[i, 4:20]

    sweeps(ub, ua, wf, ws, 1.0, 3, 21, True)

    @planes(4, 20)
    def _(x):
        c, total = plane_neighbours(ua, x, True)
        full = (1.0 - relax_weight) * c + (wf[x] + ws[x] * total)
        out[x - 4] = full[8:24]

    for halo in (rho_halo, f_halo, rho1_halo, f1_halo):
        halo.wait_send()
    for dx, dy, copy in faces:
        pl.when(has(dx, dy))(copy.wait_send)
    pltpu.make_async_copy(every, every, gsend_sem).wait()


def cycle(vectors, density):
    ns, nb = lax.axis_size("space"), lax.axis_size("sub")
    n = ns * nb
    vm = lambda *shape: pltpu.VMEM(shape, jnp.float32)
    fine, mid = (24, 32, 128), (16, 24, 128)
    return pl.pallas_call(
        functools.partial(cycle_kernel, ns, nb),
        out_shape=jax.ShapeDtypeStruct((CX, CY, CZ), jnp.float32),
        in_specs=[pl.BlockSpec(memory_space=pltpu.VMEM)] * 2,
        out_specs=pl.BlockSpec(memory_space=pltpu.VMEM),
        scratch_shapes=[
            vm(18, 16, 128), vm(16, 32, 128), vm(*fine), vm(*fine), vm(*fine), vm(*fine),
            vm(*fine), vm(*fine), vm(8, 32, 128),
            vm(*mid), vm(*mid), vm(*mid), vm(*mid), vm(*mid), vm(*mid), vm(4, 24, 128),
            vm(10, 24, 128),
            vm(8, 128), vm(n, 8, 128), vm(nb, ns * 4, 128), vm(nb, ns * 4, 128),
            vm(nb + 2, ns * 4 + 16, 128), vm(8, 8, 128),
            pltpu.SemaphoreType.DMA((36,)),
            pltpu.SemaphoreType.DMA((36,)),
            pltpu.SemaphoreType.DMA,
            pltpu.SemaphoreType.DMA,
        ],
        compiler_params=pltpu.CompilerParams(
            collective_id=0, has_side_effects=True, vmem_limit_bytes=48 * 1024 * 1024
        ),
        name="cycle",
    )(vectors, density)


def exchange_kernel(
    ns, nb, points_hbm, meta_hbm, parts, meta_out,
    points, meta, point_send, point_recv, meta_send, meta_recv, own_sem,
):
    n = ns * nb
    tiles = points_hbm.shape[2]
    me = lax.axis_index("space") * nb + lax.axis_index("sub")
    barrier = pltpu.get_barrier_semaphore()

    def where(k):
        peer = lax.rem(me + k, n)
        return peer, (peer // nb, lax.rem(peer, nb))

    def greet(k, carry):
        pl.semaphore_signal(barrier, inc=1, device_id=where(k)[1], device_id_type=MESH)
        return carry

    lax.fori_loop(1, n, greet, 0)
    own_points = pltpu.make_async_copy(points_hbm.at[me], points.at[0], own_sem.at[0])
    own_meta = pltpu.make_async_copy(meta_hbm.at[me], meta.at[0], own_sem.at[1])
    own_points.start()
    own_meta.start()
    pl.semaphore_wait(barrier, n - 1)

    def copies(k):
        peer, place = where(k)
        one = pltpu.make_async_remote_copy(
            src_ref=meta_hbm.at[peer],
            dst_ref=meta.at[k],
            send_sem=meta_send.at[k],
            recv_sem=meta_recv.at[k],
            device_id=place,
            device_id_type=MESH,
        )
        two = pltpu.make_async_remote_copy(
            src_ref=points_hbm.at[peer],
            dst_ref=points.at[k],
            send_sem=point_send.at[k],
            recv_sem=point_recv.at[k],
            device_id=place,
            device_id_type=MESH,
        )
        return one, two

    def tell(k, carry):
        for copy in copies(k):
            copy.start()
        return carry

    lax.fori_loop(1, n, tell, 0)

    centers = lax.broadcasted_iota(jnp.int32, (BRICK, 128), 0).astype(jnp.float32) + 0.5
    slot = lax.broadcasted_iota(jnp.int32, (1, 128), 1)
    left = lax.broadcasted_iota(jnp.int32, (64, 128), 1) < 64

    def split(value):
        high = value.astype(jnp.bfloat16)
        low = (value - high.astype(jnp.float32)).astype(jnp.bfloat16)
        return jnp.concatenate([high, low], axis=0)

    def factors(k, t):
        row = lambda feature: points[k, feature, t : t + 1, :]
        live = slot < meta[k, :, tiles + t : tiles + t + 1]
        wx, wy, wz = (jnp.maximum(0.0, 1.0 - jnp.abs(row(d) - centers)) for d in range(3))
        planar = jnp.concatenate([wx[i : i + 1] * wy for i in range(BRICK)], axis=0)
        loaded = jnp.concatenate(
            [jnp.where(live, row(3 + c), 0.0) * wz for c in range(4)], axis=0
        )
        return split(planar), split(loaded)

    def splat(k):
        for pair in range(tiles // 2):
            a, b = factors(k, 2 * pair), factors(k, 2 * pair + 1)
            loaded = jnp.concatenate([a[1], b[1]], axis=0)
            first, second = (
                lax.dot_general(
                    planar, loaded, (((1,), (1,)), ((), ())), preferred_element_type=jnp.float32
                )
                for planar in (a[0], b[0])
            )
            first = first[0:64] + first[64:128]
            second = second[0:64] + second[64:128]
            parts[k, pair] = jnp.where(left, first, second)

    own_meta.wait()
    own_points.wait()
    splat(0)

    def arrive(k, carry):
        one, two = copies(k)
        one.wait_recv()
        two.wait_recv()
        splat(k)
        return carry

    lax.fori_loop(1, n, arrive, 0)
    meta_out[...] = meta[...]

    def sent(k, carry):
        for copy in copies(k):
            copy.wait_send()
        return carry

    lax.fori_loop(1, n, sent, 0)


def exchange(points, meta):
    ns, nb = lax.axis_size("space"), lax.axis_size("sub")
    n, tiles = points.shape[0], points.shape[2]
    vmem = pl.BlockSpec(memory_space=pltpu.VMEM)
    return pl.pallas_call(
        functools.partial(exchange_kernel, ns, nb),
        out_shape=(
            jax.ShapeDtypeStruct((n, tiles // 2, 64, 128), jnp.float32),
            jax.ShapeDtypeStruct(meta.shape, jnp.int32),
        ),
        in_specs=[pl.BlockSpec(memory_space=pl.ANY)] * 2,
        out_specs=(vmem, vmem),
        scratch_shapes=[
            pltpu.VMEM(points.shape, jnp.float32),
            pltpu.VMEM(meta.shape, jnp.int32),
            pltpu.SemaphoreType.DMA((n,)),
            pltpu.SemaphoreType.DMA((n,)),
            pltpu.SemaphoreType.DMA((n,)),
            pltpu.SemaphoreType.DMA((n,)),
            pltpu.SemaphoreType.DMA((2,)),
        ],
        compiler_params=pltpu.CompilerParams(
            collective_id=1, has_side_effects=True, vmem_limit_bytes=48 * 1024 * 1024
        ),
        name="exchange",
    )(points, meta)


def gather_kernel(meta, parts, grid, density, acc):
    n, pairs = parts.shape[0], parts.shape[1]
    acc[...] = jnp.zeros_like(acc)
    left = lax.broadcasted_iota(jnp.int32, (64, 128), 1) < 64

    def one_peer(p, carry):
        for pair in range(pairs):
            part = parts[p, pair]
            first, second = meta[p, 0, 2 * pair], meta[p, 0, 2 * pair + 1]
            acc[first] = acc[first] + jnp.where(left, part, 0.0)
            acc[second] = acc[second] + jnp.where(left, 0.0, part)
        return carry

    lax.fori_loop(0, n, one_peer, 0, unroll=2)

    group = lax.broadcasted_iota(jnp.int32, (BRICK, 128), 1) // BRICK
    nz = CZ // BRICK

    for column in range(acc.shape[0] // nz):
        bx, by = column // (CY // BRICK), column % (CY // BRICK)

        def one_row(i, carry):
            turned = []
            for bz in range(nz):
                part = acc[column * nz + bz, pl.ds(pl.multiple_of(8 * i, 8), 8), :]
                part = part + pltpu.roll(part, 64, 1)
                part = part + pltpu.roll(part, 96, 1)
                turned.append(pltpu.roll(part, 8 * bz, 1) if bz else part)
            for c in range(4):
                value = turned[0]
                for bz in range(1, nz):
                    value = jnp.where(group == (bz + c) % nz, turned[bz], value)
                if c:
                    value = pltpu.roll(value, 128 - 8 * c, 1)
                if c < 3:
                    grid[c, BRICK * bx + i, BRICK * by : BRICK * by + BRICK, :] = value
                else:
                    density[BRICK * bx + i, BRICK * by : BRICK * by + BRICK, :] = value
            return carry

        lax.fori_loop(0, BRICK, one_row, 0, unroll=2)


def gather(meta, parts):
    bricks = CX // BRICK * (CY // BRICK) * (CZ // BRICK)
    vmem = pl.BlockSpec(memory_space=pltpu.VMEM)
    return pl.pallas_call(
        gather_kernel,
        out_shape=(
            jax.ShapeDtypeStruct((3, CX, CY, CZ), jnp.float32),
            jax.ShapeDtypeStruct((CX, CY, CZ), jnp.float32),
        ),
        in_specs=[pl.BlockSpec(memory_space=pltpu.SMEM), vmem],
        out_specs=(vmem, vmem),
        scratch_shapes=[pltpu.VMEM((bricks, 64, 128), jnp.float32)],
        compiler_params=pltpu.CompilerParams(vmem_limit_bytes=48 * 1024 * 1024),
        name="gather",
    )(meta, parts)


def on_device(offsets, normals, density, tile_brick, tile_count):
    n = lax.axis_size("space") * lax.axis_size("sub")
    tiles, slots = offsets.shape[4], offsets.shape[6]
    by_feature = lambda a: a.reshape(n, tiles, 3, slots).transpose(0, 2, 1, 3)
    points = jnp.concatenate(
        [by_feature(offsets), by_feature(normals), density.reshape(n, 1, tiles, slots)], axis=1
    )
    meta = jnp.concatenate(
        [
            tile_brick.reshape(n, 1, tiles),
            tile_count.reshape(n, 1, tiles),
            jnp.zeros((n, 1, 128 - 2 * tiles), jnp.int32),
        ],
        axis=2,
    )
    parts, meta = exchange(points, meta)
    vectors, density_field = gather(meta, parts)
    return (cycle(vectors, density_field), density_field)


def solution(mesh):
    placed = (
        P("space", "sub", None, None, None, None, None),
        P("space", "sub", None, None, None, None, None),
        P("space", "sub", None, None, None, None),
        P("space", "sub", None, None, None),
        P("space", "sub", None, None, None),
    )
    return jax.shard_map(
        on_device,
        mesh=mesh,
        in_specs=placed,
        out_specs=(P("space", "sub", None), P("space", "sub", None)),
        check_vma=False,
    )
```

```python
import functools
import math

import jax
import jax.numpy as jnp
from jax import lax
from jax.experimental import pallas as pl
from jax.experimental.pallas import tpu as pltpu
from jax.sharding import PartitionSpec as P

BRICK = 8
CX = 16
CY = 16
CZ = 128
LEVELS = 4
SWEEPS = 2
COARSE = 8


screen_weight = 0.05
relax_weight = 0.8


HX = 4
HY = 8
MESH = pl.DeviceIdType.MESH
HIGHEST = lax.Precision.HIGHEST


def dot(a, b):
    return jnp.dot(a, b, precision=HIGHEST, preferred_element_type=jnp.float32)


def grid_iota(shape):
    return lax.broadcasted_iota(jnp.int32, shape, 0), lax.broadcasted_iota(jnp.int32, shape, 1)


def modulo(value, size):
    return value & (size - 1) if size & (size - 1) == 0 else value % size


def over(value, size):
    shift = size.bit_length() - 1
    return value >> shift if size & (size - 1) == 0 else value // size


def one_where(mask, value=1.0):
    return jnp.where(mask, jnp.float32(value), jnp.float32(0.0))


def shifted_z(c, zero_ends):
    zp = pltpu.roll(c, 127, c.ndim - 1)
    zm = pltpu.roll(c, 1, c.ndim - 1)
    if zero_ends:
        lane = lax.broadcasted_iota(jnp.int32, c.shape, c.ndim - 1)
        zp = jnp.where(lane < 127, zp, 0.0)
        zm = jnp.where(lane > 0, zm, 0.0)
    return zp + zm


def plane_neighbours(ref, x, zero_ends):
    c = ref[x]
    rows = c.shape[0]
    total = ref[x - 1] + ref[x + 1]
    total = total + pltpu.roll(c, 1, 0) + pltpu.roll(c, rows - 1, 0)
    return c, total + shifted_z(c, zero_ends)


def flat_neighbours(u, xs, zl, yl):
    row, lane = grid_iota(u.shape)
    rows = u.shape[0]
    xi, zi, yi = modulo(row, xs), modulo(lane, zl), over(lane, zl)
    total = jnp.where(zi < zl - 1, pltpu.roll(u, 127, 1), 0.0)
    total = total + jnp.where(zi > 0, pltpu.roll(u, 1, 1), 0.0)
    total = total + jnp.where(xi < xs - 1, pltpu.roll(u, rows - 1, 0), 0.0)
    total = total + jnp.where(xi > 0, pltpu.roll(u, 1, 0), 0.0)
    far_up = pltpu.roll(pltpu.roll(u, zl * (yl - 1), 1), rows - xs, 0)
    far_up = jnp.where(row < rows - xs, far_up, 0.0)
    total = total + jnp.where(yi < yl - 1, pltpu.roll(u, 128 - zl, 1), far_up)
    far_down = pltpu.roll(pltpu.roll(u, 128 - zl * (yl - 1), 1), xs, 0)
    far_down = jnp.where(row >= xs, far_down, 0.0)
    return total + jnp.where(yi > 0, pltpu.roll(u, zl, 1), far_down)


class Halo:
    def __init__(self, ref, nx, ny, send, recv, base, has, place):
        self.ref, self.nx, self.ny = ref, nx, ny
        self.has = has
        self.items = []
        k = base
        for dx in (-1, 0, 1):
            for dy in (-1, 0, 1):
                if dx == 0 and dy == 0:
                    continue
                sx = {1: (nx, HX), -1: (HX, HX), 0: (HX, nx)}[dx]
                tx = {1: (0, HX), -1: (HX + nx, HX), 0: (HX, nx)}[dx]
                sy = {1: (ny, HY), -1: (HY, HY), 0: (HY, ny)}[dy]
                ty = {1: (0, HY), -1: (HY + ny, HY), 0: (HY, ny)}[dy]
                copy = pltpu.make_async_remote_copy(
                    src_ref=ref.at[pl.ds(*sx), pl.ds(*sy)],
                    dst_ref=ref.at[pl.ds(*tx), pl.ds(*ty)],
                    send_sem=send.at[k],
                    recv_sem=recv.at[k],
                    device_id=place(dx, dy),
                    device_id_type=MESH,
                )
                self.items.append((dx, dy, copy))
                k += 1

    def clear_rim(self):
        ref, nx, ny = self.ref, self.nx, self.ny

        @pl.when(jnp.logical_not(self.has(-1, 0)))
        def _():
            ref[0:HX] = jnp.zeros((HX,) + ref.shape[1:], jnp.float32)

        @pl.when(jnp.logical_not(self.has(1, 0)))
        def _():
            ref[HX + nx :] = jnp.zeros((HX,) + ref.shape[1:], jnp.float32)

        @pl.when(jnp.logical_not(self.has(0, -1)))
        def _():
            ref[:, 0:HY] = jnp.zeros((ref.shape[0], HY, 128), jnp.float32)

        @pl.when(jnp.logical_not(self.has(0, 1)))
        def _():
            ref[:, HY + ny :] = jnp.zeros((ref.shape[0], HY, 128), jnp.float32)

    def start(self):
        for dx, dy, copy in self.items:
            pl.when(self.has(dx, dy))(copy.start)

    def wait_recv(self):
        for dx, dy, copy in self.items:
            pl.when(self.has(-dx, -dy))(copy.wait_recv)

    def wait_send(self):
        for dx, dy, copy in self.items:
            pl.when(self.has(dx, dy))(copy.wait_send)


def planes(start, stop, unroll=None):
    unroll = unroll or stop - start

    def wrap(body):
        def step(x, carry):
            body(x)
            return carry

        lax.fori_loop(start, stop, step, 0, unroll=unroll)

    return wrap


def cycle_kernel(
    ns, nb, g, out,
    vxp, vyp, rhop, fp, ua, ub, wf, ws, rt,
    rho1p, f1p, u1a, u1b, wf1, ws1, rt1, pr,
    gsend, gath, f2g, rho2g, u2p, c2,
    send, recv, gsend_sem, grecv_sem,
):
    n = ns * nb
    sp, sb = lax.axis_index("space"), lax.axis_index("sub")
    me = sp * nb + sb

    def place(dx, dy):
        return (lax.rem(sp + dx + ns, ns), lax.rem(sb + dy + nb, nb))

    def has(dx, dy):
        ok = jnp.bool_(True)
        if dx:
            ok = sp + dx >= 0 if dx < 0 else sp + dx < ns
        if dy:
            oky = sb + dy >= 0 if dy < 0 else sb + dy < nb
            ok = jnp.logical_and(ok, oky) if dx else oky
        return ok

    barrier = pltpu.get_barrier_semaphore()

    def greet(k, carry):
        peer = lax.rem(me + k, n)
        pl.semaphore_signal(
            barrier, inc=1, device_id=(peer // nb, lax.rem(peer, nb)), device_id_type=MESH
        )
        return carry

    lax.fori_loop(1, n, greet, 0)

    rho_halo = Halo(rhop, 16, 16, send, recv, 0, has, place)
    f_halo = Halo(fp, 16, 16, send, recv, 8, has, place)
    rho1_halo = Halo(rho1p, 8, 8, send, recv, 16, has, place)
    f1_halo = Halo(f1p, 8, 8, send, recv, 24, has, place)

    def face(src, dst, k, dx, dy):
        return (
            dx,
            dy,
            pltpu.make_async_remote_copy(
                src_ref=src,
                dst_ref=dst,
                send_sem=send.at[k],
                recv_sem=recv.at[k],
                device_id=place(dx, dy),
                device_id_type=MESH,
            ),
        )

    faces = [
        face(vxp.at[16], vxp.at[0], 32, 1, 0),
        face(vxp.at[1], vxp.at[17], 33, -1, 0),
        face(vyp.at[:, pl.ds(16, 8)], vyp.at[:, pl.ds(0, 8)], 34, 0, 1),
        face(vyp.at[:, pl.ds(8, 8)], vyp.at[:, pl.ds(24, 8)], 35, 0, -1),
    ]
    vxp[1:17] = g[0]
    vyp[:, 8:24] = g[1]
    rhop[4:20, 8:24] = g[3]
    for halo in (rho_halo, f_halo, rho1_halo, f1_halo):
        halo.clear_rim()

    @pl.when(jnp.logical_not(has(-1, 0)))
    def _():
        vxp[0] = jnp.zeros((16, 128), jnp.float32)

    @pl.when(jnp.logical_not(has(1, 0)))
    def _():
        vxp[17] = jnp.zeros((16, 128), jnp.float32)

    @pl.when(jnp.logical_not(has(0, -1)))
    def _():
        vyp[:, 0:8] = jnp.zeros((16, 8, 128), jnp.float32)

    @pl.when(jnp.logical_not(has(0, 1)))
    def _():
        vyp[:, 24:32] = jnp.zeros((16, 8, 128), jnp.float32)

    zr, zc = grid_iota((128, 128))
    pool_z = one_where(over(zr, 2) == zc, 0.125)

    def pool_to_1(dst):
        pooled = rt[:, pl.ds(8, 8, stride=2), :] + rt[:, pl.ds(9, 8, stride=2), :]
        dst[4:12, 8:16] = dot(pooled.reshape(64, 128), pool_z).reshape(8, 8, 128)

    pool_lanes = one_where(over(zr, 2) == modulo(zc, 32), 0.125)
    prow = lax.broadcasted_iota(jnp.int32, (4, 8, 128), 1)
    plane_lane = lax.broadcasted_iota(jnp.int32, (4, 8, 128), 2)
    pick_rows = over(plane_lane, 32) == over(prow, 2)

    def pool_to_2(value):
        spread = dot(value.reshape(32, 128), pool_lanes).reshape(4, 8, 128)
        return jnp.sum(jnp.where(pick_rows, spread, 0.0), axis=1)

    pl.semaphore_wait(barrier, n - 1)
    for dx, dy, copy in faces:
        pl.when(has(dx, dy))(copy.start)
    rho_halo.start()

    @planes(0, 8)
    def _(x):
        rt[x, 8:24] = g[3, 2 * x] + g[3, 2 * x + 1]

    pool_to_1(rho1p)
    rho1_halo.start()
    for i in range(4):
        rt1[i, 8:16] = rho1p[4 + 2 * i, 8:16] + rho1p[5 + 2 * i, 8:16]
    gsend[4:8] = pool_to_2(rt1[:, 8:16])

    for dx, dy, copy in faces:
        pl.when(has(-dx, -dy))(copy.wait_recv)

    lane16 = lax.broadcasted_iota(jnp.int32, (16, 128), 1)

    @planes(0, 16)
    def _(x):
        change = vxp[x + 2] - vxp[x]
        change = change + (vyp[x, 9:25] - vyp[x, 7:23])
        vz = g[2, x]
        zp = jnp.where(lane16 < 127, pltpu.roll(vz, 127, 1), 0.0)
        zm = jnp.where(lane16 > 0, pltpu.roll(vz, 1, 1), 0.0)
        fp[x + 4, 8:24] = -0.5 * (change + (zp - zm))

    f_halo.start()
    rho_halo.wait_recv()

    def inside(x, rows, lanes, step):
        r, l = grid_iota((rows, 128))
        gx = sp * step + x - HX
        gy = sb * step + r - HY
        ok = jnp.logical_and(gy >= 0, gy < nb * step)
        ok = jnp.logical_and(ok, jnp.logical_and(gx >= 0, gx < ns * step))
        return jnp.logical_and(ok, l < lanes) if lanes < 128 else ok

    @planes(0, 24)
    def _(x):
        ws[x] = jnp.where(inside(x, 32, 128, 16), relax_weight / (6.0 + screen_weight * rhop[x]), 0.0)

    rho1_halo.wait_recv()

    @planes(0, 16)
    def _(x):
        ws1[x] = jnp.where(
            inside(x, 24, 64, 8), relax_weight / (1.5 + screen_weight * rho1p[x]), 0.0
        )

    f_halo.wait_recv()

    @planes(1, 23)
    def _(x):
        value = ws[x] * fp[x]
        wf[x] = value
        ua[x] = value

    def sweeps(src, dst, wf_ref, ws_ref, scale, start, stop, zero_ends):
        @planes(start, stop)
        def _(x):
            c, total = plane_neighbours(src, x, zero_ends)
            if scale != 1.0:
                total = scale * total
            dst[x] = (1.0 - relax_weight) * c + (wf_ref[x] + ws_ref[x] * total)

    sweeps(ua, ub, wf, ws, 1.0, 2, 22, True)

    @planes(0, 8)
    def _(x):
        parts = []
        for k in range(2):
            at = 4 + 2 * x + k
            c, total = plane_neighbours(ub, at, True)
            parts.append(fp[at] - (6.0 + screen_weight * rhop[at]) * c + total)
        rt[x] = parts[0] + parts[1]

    pool_to_1(f1p)
    f1_halo.start()
    f1_halo.wait_recv()

    @planes(0, 16)
    def _(x):
        value = ws1[x] * f1p[x]
        wf1[x] = value
        u1a[x] = value

    sweeps(u1a, u1b, wf1, ws1, 0.25, 1, 15, False)
    u1b[0] = jnp.zeros((24, 128), jnp.float32)
    u1b[15] = jnp.zeros((24, 128), jnp.float32)

    @planes(0, 4)
    def _(x):
        parts = []
        for k in range(2):
            at = 4 + 2 * x + k
            c, total = plane_neighbours(u1b, at, False)
            parts.append(f1p[at] - (1.5 + screen_weight * rho1p[at]) * c + 0.25 * total)
        rt1[x] = parts[0] + parts[1]

    gsend[0:4] = pool_to_2(rt1[:, 8:16])
    mine = sb * ns + sp

    def tell(k, carry):
        peer = lax.rem(me + k, n)
        pltpu.make_async_remote_copy(
            src_ref=gsend,
            dst_ref=gath.at[mine],
            send_sem=gsend_sem,
            recv_sem=grecv_sem,
            device_id=(peer // nb, lax.rem(peer, nb)),
            device_id_type=MESH,
        ).start()
        return carry

    lax.fori_loop(1, n, tell, 0)
    gath[mine] = gsend[...]
    u2p[...] = jnp.zeros_like(u2p)
    every = gath.at[pl.ds(0, n - 1)]
    x2, x3 = ns * 4, ns * 2
    rows2, rows3 = nb * x2, nb * x3
    r3, r2 = grid_iota((rows3, rows2))
    pool_rows = one_where(over(r2, 2) == r3)
    t2, t3 = grid_iota((rows2, rows3))
    grow_rows = one_where(over(t2, 2) == t3)
    pool_l = one_where(over(zr, 64) * 16 + over(modulo(zr, 32), 2) == zc, 0.125)
    grow_l = one_where(over(zc, 64) * 16 + over(modulo(zc, 32), 2) == zr)
    grow_z = one_where(zr == over(zc, 2))
    q0, q1 = grid_iota((128, 512))
    q_lane = modulo(q1, 128)
    grow_q = one_where(
        jnp.logical_and(
            over(q0, 32) == over(q1, 128),
            jnp.logical_and(modulo(q0, 32) == over(q_lane, 2), q_lane < 64),
        )
    )
    pltpu.make_async_copy(every, every, grecv_sem).wait()
    for b in range(nb):
        for s in range(ns):
            f2g[b, 4 * s : 4 * s + 4] = gath[b * ns + s, 0:4]
            rho2g[b, 4 * s : 4 * s + 4] = gath[b * ns + s, 4:8]
    f2 = f2g[...].reshape(rows2, 128)
    rho2 = rho2g[...].reshape(rows2, 128)
    diag2 = 0.375 + screen_weight * rho2
    w2 = relax_weight / diag2
    rho3 = dot(dot(pool_rows, rho2), pool_l)
    lane3 = grid_iota((rows3, 128))[1]
    w3 = jnp.where(lane3 < 32, relax_weight / (0.09375 + screen_weight * rho3), 0.0)

    def step2(u):
        total = flat_neighbours(u, x2, 32, 4)
        return (1.0 - relax_weight) * u + w2 * (f2 + 0.0625 * total)

    u2 = step2(w2 * f2)
    res2 = f2 - diag2 * u2 + 0.0625 * flat_neighbours(u2, x2, 32, 4)
    f3 = dot(dot(pool_rows, res2), pool_l)
    u3 = w3 * f3
    for _ in range(COARSE - 1):
        total = flat_neighbours(u3, x3, 16, 2)
        u3 = (1.0 - relax_weight) * u3 + w3 * (f3 + 0.015625 * total)
    u2 = u2 + dot(grow_rows, dot(u3, grow_l))
    u2 = step2(step2(u2))
    u2p[1 : nb + 1, 8 : 8 + x2] = u2.reshape(nb, x2, 128)

    near = [u2p[sb + o, pl.ds(4 * sp + 6, 8), :] for o in range(3)]
    fan = dot(jnp.concatenate(near, axis=0), grow_q)
    order = [(0, 2), (0, 3), (1, 0), (1, 1), (1, 2), (1, 3), (2, 0), (2, 1)]
    for at, (o, j) in enumerate(order):
        c2[:, at, :] = fan[8 * o : 8 * o + 8, 128 * j : 128 * j + 128]
    for i in range(8):
        for k in range(2):
            for m in range(2):
                rows = pl.ds(4 + m, 8, stride=2)
                u1b[2 * i + k, rows, :] = u1b[2 * i + k, rows, :] + c2[i]
    sweeps(u1b, u1a, wf1, ws1, 0.25, 2, 14, False)
    sweeps(u1a, u1b, wf1, ws1, 0.25, 3, 13, False)
    pr[...] = dot(u1b[3:13].reshape(240, 128), grow_z).reshape(10, 24, 128)

    @planes(0, 10)
    def _(i):
        for k in range(2):
            for m in range(2):
                rows = pl.ds(m, 16, stride=2)
                ub[2 * i + 2 + k, rows, :] = ub[2 * i + 2 + k, rows, :] + pr[i, 4:20]

    sweeps(ub, ua, wf, ws, 1.0, 3, 21, True)

    @planes(4, 20)
    def _(x):
        c, total = plane_neighbours(ua, x, True)
        full = (1.0 - relax_weight) * c + (wf[x] + ws[x] * total)
        out[x - 4] = full[8:24]

    for halo in (rho_halo, f_halo, rho1_halo, f1_halo):
        halo.wait_send()
    for dx, dy, copy in faces:
        pl.when(has(dx, dy))(copy.wait_send)
    pltpu.make_async_copy(every, every, gsend_sem).wait()


def cycle(grid):
    ns, nb = lax.axis_size("space"), lax.axis_size("sub")
    n = ns * nb
    vm = lambda *shape: pltpu.VMEM(shape, jnp.float32)
    fine, mid = (24, 32, 128), (16, 24, 128)
    return pl.pallas_call(
        functools.partial(cycle_kernel, ns, nb),
        out_shape=jax.ShapeDtypeStruct((CX, CY, CZ), jnp.float32),
        in_specs=[pl.BlockSpec(memory_space=pltpu.VMEM)],
        out_specs=pl.BlockSpec(memory_space=pltpu.VMEM),
        scratch_shapes=[
            vm(18, 16, 128), vm(16, 32, 128), vm(*fine), vm(*fine), vm(*fine), vm(*fine),
            vm(*fine), vm(*fine), vm(8, 32, 128),
            vm(*mid), vm(*mid), vm(*mid), vm(*mid), vm(*mid), vm(*mid), vm(4, 24, 128),
            vm(10, 24, 128),
            vm(8, 128), vm(n, 8, 128), vm(nb, ns * 4, 128), vm(nb, ns * 4, 128),
            vm(nb + 2, ns * 4 + 16, 128), vm(8, 8, 128),
            pltpu.SemaphoreType.DMA((36,)),
            pltpu.SemaphoreType.DMA((36,)),
            pltpu.SemaphoreType.DMA,
            pltpu.SemaphoreType.DMA,
        ],
        compiler_params=pltpu.CompilerParams(
            collective_id=0, has_side_effects=True, vmem_limit_bytes=48 * 1024 * 1024
        ),
        name="cycle",
    )(grid)


def exchange_kernel(
    ns, nb, points_hbm, meta_hbm, parts, meta_out,
    points, meta, point_send, point_recv, meta_send, meta_recv, own_sem,
):
    n = ns * nb
    tiles = points_hbm.shape[2]
    me = lax.axis_index("space") * nb + lax.axis_index("sub")
    barrier = pltpu.get_barrier_semaphore()

    def where(k):
        peer = lax.rem(me + k, n)
        return peer, (peer // nb, lax.rem(peer, nb))

    def greet(k, carry):
        pl.semaphore_signal(barrier, inc=1, device_id=where(k)[1], device_id_type=MESH)
        return carry

    lax.fori_loop(1, n, greet, 0)
    own_points = pltpu.make_async_copy(points_hbm.at[me], points.at[0], own_sem.at[0])
    own_meta = pltpu.make_async_copy(meta_hbm.at[me], meta.at[0], own_sem.at[1])
    own_points.start()
    own_meta.start()
    pl.semaphore_wait(barrier, n - 1)

    def copies(k):
        peer, place = where(k)
        one = pltpu.make_async_remote_copy(
            src_ref=meta_hbm.at[peer],
            dst_ref=meta.at[k],
            send_sem=meta_send.at[k],
            recv_sem=meta_recv.at[k],
            device_id=place,
            device_id_type=MESH,
        )
        two = pltpu.make_async_remote_copy(
            src_ref=points_hbm.at[peer],
            dst_ref=points.at[k],
            send_sem=point_send.at[k],
            recv_sem=point_recv.at[k],
            device_id=place,
            device_id_type=MESH,
        )
        return one, two

    def tell(k, carry):
        for copy in copies(k):
            copy.start()
        return carry

    lax.fori_loop(1, n, tell, 0)

    centers = lax.broadcasted_iota(jnp.int32, (BRICK, 128), 0).astype(jnp.float32) + 0.5
    slot = lax.broadcasted_iota(jnp.int32, (1, 128), 1)
    left = lax.broadcasted_iota(jnp.int32, (64, 128), 1) < 64

    def split(value):
        high = value.astype(jnp.bfloat16)
        low = (value - high.astype(jnp.float32)).astype(jnp.bfloat16)
        return jnp.concatenate([high, low], axis=0)

    def factors(k, t):
        row = lambda feature: points[k, feature, t : t + 1, :]
        live = slot < meta[k, :, tiles + t : tiles + t + 1]
        wx, wy, wz = (jnp.maximum(0.0, 1.0 - jnp.abs(row(d) - centers)) for d in range(3))
        planar = jnp.concatenate([wx[i : i + 1] * wy for i in range(BRICK)], axis=0)
        loaded = jnp.concatenate(
            [jnp.where(live, row(3 + c), 0.0) * wz for c in range(4)], axis=0
        )
        return split(planar), split(loaded)

    def splat(k):
        for pair in range(tiles // 2):
            a, b = factors(k, 2 * pair), factors(k, 2 * pair + 1)
            loaded = jnp.concatenate([a[1], b[1]], axis=0)
            first, second = (
                lax.dot_general(
                    planar, loaded, (((1,), (1,)), ((), ())), preferred_element_type=jnp.float32
                )
                for planar in (a[0], b[0])
            )
            first = first[0:64] + first[64:128]
            second = second[0:64] + second[64:128]
            parts[k, pair] = jnp.where(left, first, second)

    width = math.gcd(n, 4)

    def land(k):
        for copy in copies(k):
            copy.wait_recv()

    own_meta.wait()
    own_points.wait()
    for k in range(1, width):
        land(k)
    for k in range(width):
        splat(k)

    def arrive(group, carry):
        for k in range(width):
            land(group * width + k)
        for k in range(width):
            splat(group * width + k)
        return carry

    lax.fori_loop(1, n // width, arrive, 0)
    meta_out[...] = meta[...]

    def sent(k, carry):
        for copy in copies(k):
            copy.wait_send()
        return carry

    lax.fori_loop(1, n, sent, 0)


def exchange(points, meta):
    ns, nb = lax.axis_size("space"), lax.axis_size("sub")
    n, tiles = points.shape[0], points.shape[2]
    vmem = pl.BlockSpec(memory_space=pltpu.VMEM)
    return pl.pallas_call(
        functools.partial(exchange_kernel, ns, nb),
        out_shape=(
            jax.ShapeDtypeStruct((n, tiles // 2, 64, 128), jnp.float32),
            jax.ShapeDtypeStruct(meta.shape, jnp.int32),
        ),
        in_specs=[pl.BlockSpec(memory_space=pl.ANY)] * 2,
        out_specs=(vmem, vmem),
        scratch_shapes=[
            pltpu.VMEM(points.shape, jnp.float32),
            pltpu.VMEM(meta.shape, jnp.int32),
            pltpu.SemaphoreType.DMA((n,)),
            pltpu.SemaphoreType.DMA((n,)),
            pltpu.SemaphoreType.DMA((n,)),
            pltpu.SemaphoreType.DMA((n,)),
            pltpu.SemaphoreType.DMA((2,)),
        ],
        compiler_params=pltpu.CompilerParams(
            collective_id=1, has_side_effects=True, vmem_limit_bytes=48 * 1024 * 1024
        ),
        name="exchange",
    )(points, meta)


def gather_kernel(meta, parts, grid, density, acc, acd):
    n, pairs = parts.shape[0], parts.shape[1]
    acc[...] = jnp.zeros_like(acc)
    acd[...] = jnp.zeros_like(acd)
    left = lax.broadcasted_iota(jnp.int32, (BRICK, 128), 1) < 64

    def one_peer(p, carry):
        for pair in range(pairs):
            part = parts[p, pair]
            first, second = meta[p, 0, 2 * pair], meta[p, 0, 2 * pair + 1]
            acc[first] = acc[first] + part
            acd[second] = acd[second] + part
        return carry

    lax.fori_loop(0, n, one_peer, 0, unroll=2)

    group = lax.broadcasted_iota(jnp.int32, (BRICK, 128), 1) // BRICK
    nz = CZ // BRICK

    for column in range(acc.shape[0] // nz):
        bx, by = column // (CY // BRICK), column % (CY // BRICK)

        def one_row(i, carry):
            values = [None] * 4
            rows = pl.ds(pl.multiple_of(8 * i, 8), 8)
            for bz in range(nz):
                brick = column * nz + bz
                part = jnp.where(left, acc[brick, rows, :], acd[brick, rows, :])
                part = part + pltpu.roll(part, 64, 1)
                part = part + pltpu.roll(part, 96, 1)
                part = pltpu.roll(part, 8 * bz, 1) if bz else part
                for c in range(4):
                    values[c] = jnp.where(group == (bz + c) % nz, part, values[c]) if bz else part
            for c in range(4):
                value = pltpu.roll(values[c], 128 - 8 * c, 1) if c else values[c]
                grid[c, BRICK * bx + i, BRICK * by : BRICK * by + BRICK, :] = value
                if c == 3:
                    density[BRICK * bx + i, BRICK * by : BRICK * by + BRICK, :] = value
            return carry

        lax.fori_loop(0, BRICK, one_row, 0, unroll=4)


def gather(meta, parts):
    bricks = CX // BRICK * (CY // BRICK) * (CZ // BRICK)
    vmem = pl.BlockSpec(memory_space=pltpu.VMEM)
    return pl.pallas_call(
        gather_kernel,
        out_shape=(
            jax.ShapeDtypeStruct((4, CX, CY, CZ), jnp.float32),
            jax.ShapeDtypeStruct((CX, CY, CZ), jnp.float32),
        ),
        in_specs=[pl.BlockSpec(memory_space=pltpu.SMEM), vmem],
        out_specs=(vmem, vmem),
        scratch_shapes=[pltpu.VMEM((bricks, 64, 128), jnp.float32)] * 2,
        compiler_params=pltpu.CompilerParams(vmem_limit_bytes=48 * 1024 * 1024),
        name="gather",
    )(meta, parts)


def on_device(offsets, normals, density, tile_brick, tile_count):
    n = lax.axis_size("space") * lax.axis_size("sub")
    tiles, slots = offsets.shape[4], offsets.shape[6]
    by_feature = lambda a: a.reshape(n, tiles, 3, slots).transpose(0, 2, 1, 3)
    points = jnp.concatenate(
        [by_feature(offsets), by_feature(normals), density.reshape(n, 1, tiles, slots)], axis=1
    )
    meta = jnp.concatenate(
        [
            tile_brick.reshape(n, 1, tiles),
            tile_count.reshape(n, 1, tiles),
            jnp.zeros((n, 1, 128 - 2 * tiles), jnp.int32),
        ],
        axis=2,
    )
    parts, meta = exchange(points, meta)
    grid, density_field = gather(meta, parts)
    return (cycle(grid), density_field)


def solution(mesh):
    placed = (
        P("space", "sub", None, None, None, None, None),
        P("space", "sub", None, None, None, None, None),
        P("space", "sub", None, None, None, None),
        P("space", "sub", None, None, None),
        P("space", "sub", None, None, None),
    )
    return jax.shard_map(
        on_device,
        mesh=mesh,
        in_specs=placed,
        out_specs=(P("space", "sub", None), P("space", "sub", None)),
        check_vma=False,
    )
```
